32 devices in a mesh: node: 4 (over z), event: 8 (over y, x, core).
Axes of the slice: x: 2, y: 2, z: 4, core: 2. Of those that a mesh axis runs over, the one named last changes fastest.
Arguments:
- memory: bfloat16 [8192, 256], P('node'), may hold values from -6 to 6
- event_feat: bfloat16 [32, 32, 16, 128], P(('node', 'event')), may hold values from -6 to 6
- event_source: int32 [32, 32, 16], P(('node', 'event')), may hold values from 0 to 2047
- event_partner: int32 [32, 32, 16], P(('node', 'event')), may hold values from 0 to 511
- event_negative: int32 [32, 32, 16], P(('node', 'event')), may hold values from 0 to 511
- event_time: int32 [32, 32, 16], P(('node', 'event')), may hold values from 0 to 1023
- event_count: int32 [32, 32], P(('node', 'event')), may hold values from 0 to 16, as said below
- requests: int32 [32, 4, 128], P(('node', 'event')), may hold values from 0 to 2047
- w_input: bfloat16 [512, 768], replicated, may hold values from -0.25 to 0.25
- w_state: bfloat16 [256, 768], replicated, may hold values from -0.375 to 0.375
- w_pair: bfloat16 [256, 256], replicated, may hold values from -0.375 to 0.375
- gate_bias: float32 [768], replicated, may hold values from -3 to 3
- time_freq: float32 [128], replicated, may hold values from 0.001 to 1
Outputs:
- memory_grad: float32 [8192, 256], P(('node', 'event'))
The draws below stay inside these ranges and needn't reach their ends.
Inputs may be any that keep to these rules, and one draw needn't show every extreme that they name: `event_count`: in every draw some device receives 16 live slots from every time block.
All inputs are finite; a program needn't handle non-finite values.
Results may differ from the reference program's by a relative error of at most 0.0021.
Values may be sent and summed in bfloat16 or wider, within the bound.
A program may use at most 64 MiB of HBM per device.

```python
import math
import jax
import jax.numpy as jnp
from jax import lax

DM = 256
EF = 128
TE = 128
TBINS = 1024
CAP = 16
PCAP = 128
NODE_GRP = 2048
SHARDS = 32
NODES = 8192
TABLE = 512
DIN = 512
N_NODE = 4
N_EVENT = 8


def draw_event_count(key, part):
    first = jax.random.fold_in(key, 11)
    second = jax.random.fold_in(key, 12)
    third = jax.random.fold_in(key, 13)
    base = jax.random.randint(first, (SHARDS, SHARDS), 0, CAP + 1)
    weight = jax.random.randint(second, (1, SHARDS), 1, 5)
    counts = jnp.minimum(CAP, base * weight // 2)
    full = jax.random.randint(third, (), 0, SHARDS)
    column = jnp.arange(SHARDS, dtype=jnp.int32)[None, :] == full
    return jnp.where(column, CAP, counts).astype(jnp.int32)


def with_ends(array, stream_key, least, top_value):
    extent = array.shape
    place = [jax.random.randint(jax.random.fold_in(stream_key, axis), (), 0, extent[axis]) for axis in range(len(extent))]
    array = array.at[tuple(place)].set(least)
    longest = extent.index(max(extent))
    place[longest] = (place[longest] + 1) % extent[longest]
    return array.at[tuple(place)].set(top_value)


def level_of(key, shape, shards, least, largest):
    gain, own = 1.0, jax.random.fold_in(key, 6)
    for axis_at, blocks in shards:
        heights = jnp.exp(jax.random.uniform(jax.random.fold_in(own, axis_at), (blocks,), jnp.float32, least / len(shards), largest / len(shards)))
        gain = gain * jnp.repeat(heights, shape[axis_at] // blocks).reshape([-1 if axis == axis_at else 1 for axis in range(len(shape))])
    return gain


def gaussian(own_key, dims, scale, bound, pieces=(), held_as=jnp.bfloat16):
    drawn = scale * jax.random.normal(own_key, dims, jnp.float32)
    if pieces:
        drawn = drawn * level_of(own_key, dims, pieces, -0.22, 0.18)
    return jnp.clip(drawn, -bound, bound).astype(held_as)


def setup_inputs(seed: int = 0) -> dict:
    seeds = jax.random.split(jax.random.key(seed), 14)
    memory = gaussian(seeds[0], (NODES, DM), 1.0, 6.0, ((0, 4),))
    event_feat = gaussian(seeds[1], (SHARDS, SHARDS, CAP, EF), 1.0, 6.0, ((0, 32),))
    event_source = with_ends(jax.random.randint(seeds[2], (SHARDS, SHARDS, CAP), 0, NODE_GRP), jax.random.fold_in(seeds[2], 1), 0, NODE_GRP - 1).astype(jnp.int32)
    event_partner = with_ends(jax.random.randint(seeds[3], (SHARDS, SHARDS, CAP), 0, TABLE), jax.random.fold_in(seeds[3], 1), 0, TABLE - 1).astype(jnp.int32)
    event_negative = with_ends(jax.random.randint(seeds[4], (SHARDS, SHARDS, CAP), 0, TABLE), jax.random.fold_in(seeds[4], 1), 0, TABLE - 1).astype(jnp.int32)
    event_time = with_ends(jax.random.randint(seeds[5], (SHARDS, SHARDS, CAP), 0, TBINS), jax.random.fold_in(seeds[5], 1), 0, TBINS - 1).astype(jnp.int32)
    event_count = draw_event_count(jax.random.fold_in(seeds[13], 71), 0)
    requests = with_ends(jax.random.randint(seeds[7], (SHARDS, N_NODE, PCAP), 0, NODE_GRP), jax.random.fold_in(seeds[7], 1), 0, NODE_GRP - 1).astype(jnp.int32)
    w_input = gaussian(seeds[8], (DIN, 3 * DM), DIN ** -0.5, 0.25)
    w_state = gaussian(seeds[9], (DM, 3 * DM), DM ** -0.5, 0.375)
    w_pair = gaussian(seeds[10], (DM, DM), DM ** -0.5, 0.375)
    gate_bias = gaussian(seeds[11], (3 * DM,), 0.5, 3.0, (), jnp.float32)
    time_freq = jnp.clip(jnp.exp(jax.random.uniform(seeds[12], (TE,), jnp.float32, math.log(0.001), math.log(1.0))), 0.001, 1.0)
    return {"memory": memory, "event_feat": event_feat, "event_source": event_source, "event_partner": event_partner, "event_negative": event_negative, "event_time": event_time, "event_count": event_count, "requests": requests, "w_input": w_input, "w_state": w_state, "w_pair": w_pair, "gate_bias": gate_bias, "time_freq": time_freq}


def pair_grads(current, partner, negative, feature, timing, valid, w_input, w_state, w_pair, gate_bias):
    width = current.shape[1]
    joined = jnp.concatenate([partner, feature, timing], axis=1)
    from_input = jnp.dot(joined, w_input, preferred_element_type=jnp.float32)
    from_state = jnp.dot(current, w_state, preferred_element_type=jnp.float32)
    reset = jax.nn.sigmoid(from_input[:, :width] + from_state[:, :width] + gate_bias[:width])
    update = jax.nn.sigmoid(from_input[:, width:2 * width] + from_state[:, width:2 * width] + gate_bias[width:2 * width])
    recurrent = from_state[:, 2 * width:]
    candidate = jnp.tanh(from_input[:, 2 * width:] + gate_bias[2 * width:] + reset * recurrent)
    previous = current.astype(jnp.float32)
    renewed = (1.0 - update) * candidate + update * previous
    factor = 1.0 / math.sqrt(width)
    key_pos = jnp.dot(partner, w_pair, preferred_element_type=jnp.float32)
    key_neg = jnp.dot(negative, w_pair, preferred_element_type=jnp.float32)
    score_pos = lax.optimization_barrier(jnp.sum(renewed * key_pos, axis=1)) * factor
    score_neg = lax.optimization_barrier(jnp.sum(renewed * key_neg, axis=1)) * factor
    weight_pos = -valid * jax.nn.sigmoid(-score_pos)
    weight_neg = valid * jax.nn.sigmoid(score_neg)
    grad_renewed = (weight_pos[:, None] * key_pos + weight_neg[:, None] * key_neg) * factor
    grad_keypos = (weight_pos[:, None] * renewed * factor).astype(jnp.bfloat16)
    grad_keyneg = (weight_neg[:, None] * renewed * factor).astype(jnp.bfloat16)
    grad_cand = grad_renewed * (1.0 - update) * (1.0 - candidate * candidate)
    grad_reset = grad_cand * recurrent * reset * (1.0 - reset)
    grad_update = grad_renewed * (previous - candidate) * update * (1.0 - update)
    input_back = jnp.concatenate([grad_reset, grad_update, grad_cand], axis=1).astype(jnp.bfloat16)
    state_back = jnp.concatenate([grad_reset, grad_update, grad_cand * reset], axis=1).astype(jnp.bfloat16)
    through_input = jnp.dot(input_back, w_input.T, preferred_element_type=jnp.float32)
    grad_current = grad_renewed * update + jnp.dot(state_back, w_state.T, preferred_element_type=jnp.float32)
    grad_partner = through_input[:, :width] + jnp.dot(grad_keypos, w_pair.T, preferred_element_type=jnp.float32)
    grad_negative = jnp.dot(grad_keyneg, w_pair.T, preferred_element_type=jnp.float32)
    return (grad_current, grad_partner, grad_negative)

def reference(memory, event_feat, event_source, event_partner, event_negative, event_time, event_count, requests, w_input, w_state, w_pair, gate_bias, time_freq):
    slots = SHARDS * CAP
    owners = jnp.arange(N_NODE, dtype=jnp.int32)[:, None] * NODE_GRP
    table_ids = (owners[None, :, :] + requests).reshape(SHARDS, N_NODE * PCAP)
    column = jnp.arange(CAP, dtype=jnp.int32)

    def one_device(total, target):
        feature = event_feat[:, target].reshape(slots, EF)
        group = target // N_EVENT
        source_ids = group * NODE_GRP + event_source[:, target].reshape(slots)
        listed = table_ids[target]
        partner_ids = listed[event_partner[:, target].reshape(slots)]
        negative_ids = listed[event_negative[:, target].reshape(slots)]
        timing = jnp.cos(event_time[:, target].reshape(slots).astype(jnp.float32)[:, None] * time_freq[None, :]).astype(jnp.bfloat16)
        valid = (column[None, :] < event_count[:, target][:, None]).astype(jnp.float32).reshape(slots)
        grad_current, grad_partner, grad_negative = pair_grads(memory[source_ids], memory[partner_ids], memory[negative_ids], feature, timing, valid, w_input, w_state, w_pair, gate_bias)
        total = total.at[source_ids].add(grad_current)
        total = total.at[partner_ids].add(grad_partner)
        total = total.at[negative_ids].add(grad_negative)
        return (total, None)
    total, _ = lax.scan(one_device, jnp.zeros((NODES, DM), jnp.float32), jnp.arange(SHARDS, dtype=jnp.int32))
    return total
```

```python
import functools
import math

import jax
import jax.numpy as jnp
from jax import lax
from jax.experimental import pallas as pl
from jax.experimental.pallas import tpu as pltpu
from jax.sharding import PartitionSpec as P

MESH = pl.DeviceIdType.MESH
BF = jnp.bfloat16
F32 = jnp.float32
LANES = 128


def mm(a, b):
    return jnp.dot(a, b, preferred_element_type=F32)


def mm_nt(a, b):
    return lax.dot_general(a, b, (((1,), (1,)), ((), ())), preferred_element_type=F32)


def split(value):
    high = value.astype(BF)
    return high, (value - high.astype(F32)).astype(BF)


def one_hot(mask):
    return jnp.where(mask, 1.0, 0.0).astype(BF)


def pick_matrix(column, total):
    lane = lax.broadcasted_iota(jnp.int32, column.shape, 1)
    return jnp.concatenate(
        [one_hot(column == lane + start) for start in range(0, total, LANES)], axis=1
    )


def spread_matrix(row, total, base):
    ids = lax.broadcasted_iota(jnp.int32, (total, row.shape[1]), 0) + base
    return one_hot(ids == row)


def kernel(
    n_node,
    n_event,
    chunk,
    pack_ref,
    feat_ref,
    req_ref,
    mem_hbm,
    win_hbm,
    wst_hbm,
    wpair_hbm,
    bias_ref,
    freq_ref,
    out_ref,
    mem,
    win,
    wst,
    wpair,
    feats,
    packs,
    wanted,
    fetched,
    table,
    pre,
    recur,
    prev,
    ids_row,
    ids_col,
    table_grad,
    cur_high,
    cur_low,
    back_out,
    back_in,
    own_low,
    acc,
    pair_out,
    pair_in,
    block_out,
    block_in,
    load_sem,
    feat_send,
    feat_recv,
    pack_send,
    pack_recv,
    req_send,
    req_recv,
    tab_send,
    tab_recv,
    back_send,
    back_recv,
    pair_send,
    pair_recv,
    block_send,
    block_recv,
):
    shards = n_node * n_event
    node, event = lax.axis_index("node"), lax.axis_index("event")
    me = node * n_event + event
    slots = feat_ref.shape[1]
    width = mem.shape[1]
    group_rows = mem.shape[0]
    asked = req_ref.shape[2]
    table_rows = n_node * asked
    events = shards * slots
    turns = events // chunk
    chips = n_event // 2
    chip, core = event // 2, event % 2
    sibling = event + 1 - 2 * core
    block = group_rows // n_event

    barrier = pltpu.get_barrier_semaphore()

    @pl.loop(1, shards)
    def _(k):
        peer = lax.rem(me + k, shards)
        pl.semaphore_signal(
            barrier, inc=1, device_id=(peer // n_event, peer % n_event), device_id_type=MESH
        )

    loads = [
        pltpu.make_async_copy(mem_hbm, mem, load_sem.at[0]),
        pltpu.make_async_copy(win_hbm, win, load_sem.at[1]),
        pltpu.make_async_copy(wst_hbm, wst, load_sem.at[2]),
        pltpu.make_async_copy(wpair_hbm, wpair, load_sem.at[3]),
    ]
    for load in loads:
        load.start()
    own_feat = pltpu.make_async_copy(feat_ref.at[me], feats.at[me], feat_recv)
    own_feat.start()
    packs[me] = pack_ref[me]
    wanted[node] = req_ref[node]
    pl.semaphore_wait(barrier, shards - 1)

    def to_node(k):
        return lax.rem(node + k, n_node)

    def request_copy(k):
        peer = to_node(k)
        return pltpu.make_async_remote_copy(
            src_ref=req_ref.at[peer],
            dst_ref=wanted.at[node],
            send_sem=req_send.at[peer],
            recv_sem=req_recv.at[node],
            device_id=(peer, event),
            device_id_type=MESH,
        )

    for k in range(1, n_node):
        request_copy(k).start()

    @pl.loop(1, shards)
    def _(k):
        peer = lax.rem(me + k, shards)
        target = (peer // n_event, peer % n_event)
        pltpu.make_async_remote_copy(
            src_ref=pack_ref.at[peer],
            dst_ref=packs.at[me],
            send_sem=pack_send,
            recv_sem=pack_recv,
            device_id=target,
            device_id_type=MESH,
        ).start()
        pltpu.make_async_remote_copy(
            src_ref=feat_ref.at[peer],
            dst_ref=feats.at[me],
            send_sem=feat_send,
            recv_sem=feat_recv,
            device_id=target,
            device_id_type=MESH,
        ).start()

    def arrived(buffer, sem, slot):
        pltpu.make_async_copy(buffer.at[slot], buffer.at[slot], sem.at[slot]).wait()

    for k in range(1, n_node):
        arrived(wanted, req_recv, to_node(k))
    loads[0].wait()
    rows = []
    for g in range(n_node):
        spread = jnp.broadcast_to(wanted[g], (LANES, asked))
        rows.append(spread.T)
    picked = mm(pick_matrix(jnp.concatenate(rows, axis=0), group_rows), mem[...]).astype(BF)
    fetched[...] = picked.reshape(n_node, asked, width)

    def table_copy(k):
        peer = to_node(k)
        return pltpu.make_async_remote_copy(
            src_ref=fetched.at[peer],
            dst_ref=table.at[node],
            send_sem=tab_send.at[peer],
            recv_sem=tab_recv.at[node],
            device_id=(peer, event),
            device_id_type=MESH,
        )

    for k in range(n_node - 1, 0, -1):
        table_copy(k).start()
    table[node] = fetched[node]

    pltpu.make_async_copy(feats, feats, feat_recv).wait()
    others = packs.at[pl.ds(0, shards - 1)]
    pltpu.make_async_copy(others, others, pack_recv).wait()
    for load in loads[1:]:
        load.wait()
    codes = packs[...].reshape(shards, LANES)
    code_parts = jnp.concatenate([codes >> 8, codes & 255], axis=1).astype(F32).astype(BF)
    kinds = 5
    from_lane = lax.broadcasted_iota(jnp.int32, (2 * LANES, kinds * LANES), 0)
    to_kind = lax.broadcasted_iota(jnp.int32, (2 * LANES, kinds * LANES), 1) // LANES
    weight = jnp.where(from_lane < LANES, 256.0, 1.0)
    gather_kind = jnp.where((from_lane % LANES) // slots == to_kind, weight, 0.0).astype(BF)

    @pl.loop(0, turns)
    def _(t):
        first = t * (chunk // slots)
        home = lax.broadcasted_iota(jnp.int32, (chunk, shards), 0) // slots + first
        from_home = one_hot(home == lax.broadcasted_iota(jnp.int32, (chunk, shards), 1))
        mine = mm(from_home, code_parts)
        lane = lax.broadcasted_iota(jnp.int32, (chunk, 2 * LANES), 1)
        slot = lax.broadcasted_iota(jnp.int32, (chunk, 2 * LANES), 0)
        mine = jnp.where(lane % slots == slot % slots, mine, 0.0).astype(BF)
        columns = mm(mine, gather_kind)
        times = columns[:, 3 * LANES : 4 * LANES]
        ids_col[t, 0] = columns[:, LANES : 2 * LANES].astype(jnp.int32)
        ids_col[t, 1] = columns[:, 2 * LANES : 3 * LANES].astype(jnp.int32)
        ids_col[t, 2] = columns[:, 4 * LANES :].astype(jnp.int32)
        for kind in range(3):
            line = columns[:, kind * LANES : (kind + 1) * LANES].T
            ids_row[t, kind] = line[:8].astype(jnp.int32)
        source = columns[:, :LANES].astype(jnp.int32)
        current = mm(pick_matrix(source, group_rows), mem[...]).astype(BF)
        from_state = mm(current, wst[...])
        timing = jnp.cos(times * freq_ref[...]).astype(BF)
        feature = feats[pl.ds(first, chunk // slots)].reshape(chunk, feat_ref.shape[2])
        from_rest = mm(jnp.concatenate([feature, timing], axis=1), win[width:, :])
        prev[t] = current
        recur[t] = from_state[:, 2 * width :]
        gates = from_rest[:, : 2 * width] + from_state[:, : 2 * width]
        pre[t] = jnp.concatenate([gates, from_rest[:, 2 * width :]], axis=1) + bias_ref[...]

    for k in range(1, n_node):
        arrived(table, tab_recv, to_node(k))
    table_grad[...] = jnp.zeros_like(table_grad)
    factor = 1.0 / math.sqrt(width)

    @pl.loop(0, turns)
    def _(t):
        rows_held = table[...].reshape(table_rows, width)
        partner = mm(pick_matrix(ids_col[t, 0], table_rows), rows_held).astype(BF)
        negative = mm(pick_matrix(ids_col[t, 1], table_rows), rows_held).astype(BF)
        valid = ids_col[t, 2].astype(F32)[:, :1]
        all_pre = pre[t] + mm(partner, win[:width, :])
        recurrent = recur[t]
        previous = prev[t].astype(F32)
        reset = jax.nn.sigmoid(all_pre[:, :width])
        update = jax.nn.sigmoid(all_pre[:, width : 2 * width])
        candidate = jnp.tanh(all_pre[:, 2 * width :] + reset * recurrent)
        renewed = (1.0 - update) * candidate + update * previous
        key_pos = mm(partner, wpair[...])
        key_neg = mm(negative, wpair[...])
        score_pos = jnp.sum(renewed * key_pos, axis=1, keepdims=True) * factor
        score_neg = jnp.sum(renewed * key_neg, axis=1, keepdims=True) * factor
        weight_pos = -valid * jax.nn.sigmoid(-score_pos)
        weight_neg = valid * jax.nn.sigmoid(score_neg)
        grad_renewed = (weight_pos * key_pos + weight_neg * key_neg) * factor
        grad_keypos = (weight_pos * renewed * factor).astype(BF)
        grad_keyneg = (weight_neg * renewed * factor).astype(BF)
        grad_cand = grad_renewed * (1.0 - update) * (1.0 - candidate * candidate)
        grad_reset = (grad_cand * recurrent * reset * (1.0 - reset)).astype(BF)
        grad_update = (
            grad_renewed * (previous - candidate) * update * (1.0 - update)
        ).astype(BF)
        input_back = jnp.concatenate([grad_reset, grad_update, grad_cand.astype(BF)], axis=1)
        state_back = jnp.concatenate(
            [grad_reset, grad_update, (grad_cand * reset).astype(BF)], axis=1
        )
        grad_partner = mm_nt(input_back, win[:width, :]) + mm_nt(grad_keypos, wpair[...])
        grad_negative = mm_nt(grad_keyneg, wpair[...])
        high, low = split(jnp.concatenate([grad_partner, grad_negative], axis=0))
        spread = jnp.concatenate(
            [
                spread_matrix(ids_row[t, 1][:1], table_rows, 0),
                spread_matrix(ids_row[t, 2][:1], table_rows, 0),
            ],
            axis=1,
        )
        table_grad[...] += mm(spread, high) + mm(spread, low)
        grad_current = grad_renewed * update + mm_nt(state_back, wst[...])
        high, low = split(grad_current)
        cur_high[t] = high
        cur_low[t] = low

    high, low = split(table_grad[...])
    back_out[...] = high.reshape(n_node, asked, width)

    def back_copy(k):
        peer = to_node(k)
        return pltpu.make_async_remote_copy(
            src_ref=back_out.at[peer],
            dst_ref=back_in.at[node],
            send_sem=back_send.at[peer],
            recv_sem=back_recv.at[node],
            device_id=(peer, event),
            device_id_type=MESH,
        )

    for k in range(n_node - 1, 0, -1):
        back_copy(k).start()
    table_grad[...] = low.astype(F32)
    own_low[...] = table_grad[pl.ds(pl.multiple_of(node * asked, asked), asked), :].astype(BF)
    back_in[node] = back_out[node]

    @pl.loop(0, n_event)
    def _(b):
        total = mm(spread_matrix(wanted[node], block, b * block), own_low[...])
        for t in range(turns):
            spread = spread_matrix(ids_row[t, 0][:1], block, b * block)
            total += mm(spread, cur_high[t]) + mm(spread, cur_low[t])
        acc[b] = total

    for k in range(1, n_node):
        arrived(back_in, back_recv, to_node(k))
    returned = back_in[...].reshape(table_rows, width)
    listed = jnp.concatenate([wanted[g] for g in range(n_node)], axis=1)

    def whole_block(b):
        return acc[b] + mm(spread_matrix(listed, block, b * block), returned)

    def pair_copy(j):
        return pltpu.make_async_remote_copy(
            src_ref=pair_out.at[j],
            dst_ref=pair_in.at[j],
            send_sem=pair_send.at[j],
            recv_sem=pair_recv.at[j],
            device_id=(node, sibling),
            device_id_type=MESH,
        )

    def block_copy(j):
        return pltpu.make_async_remote_copy(
            src_ref=block_out.at[j],
            dst_ref=block_in.at[chip],
            send_sem=block_send.at[j],
            recv_sem=block_recv.at[chip],
            device_id=(node, 2 * j + core),
            device_id_type=MESH,
        )

    @pl.loop(1, chips + 1)
    def _(k):
        j = lax.rem(chip + k, chips)
        pair_out[j] = whole_block(2 * j + 1 - core)
        pair_copy(j).start()

    @pl.loop(1, chips)
    def _(k):
        j = lax.rem(chip + k, chips)
        total = whole_block(2 * j + core)
        arrived(pair_in, pair_recv, j)
        block_out[j] = (total + pair_in[j]).astype(BF)
        block_copy(j).start()

    total = whole_block(event)
    arrived(pair_in, pair_recv, chip)
    total += pair_in[chip]
    for k in range(1, chips):
        j = lax.rem(chip + k, chips)
        arrived(block_in, block_recv, j)
        total += block_in[j].astype(F32)
    out_ref[...] = total

    for k in range(1, n_node):
        request_copy(k).wait_send()
        table_copy(k).wait_send()
        back_copy(k).wait_send()
    for k in range(1, chips):
        block_copy(lax.rem(chip + k, chips)).wait_send()
    for j in range(chips):
        pair_copy(j).wait_send()
    sent = feats.at[pl.ds(0, shards - 1)]
    pltpu.make_async_copy(sent, sent, feat_send).wait()
    pltpu.make_async_copy(others, others, pack_send).wait()


def local(
    memory,
    event_feat,
    event_source,
    event_partner,
    event_negative,
    event_time,
    event_count,
    requests,
    w_input,
    w_state,
    w_pair,
    gate_bias,
    time_freq,
):
    n_node = lax.axis_size("node")
    n_event = lax.axis_size("event")
    shards = n_node * n_event
    slots, feat_width = event_feat.shape[2:]
    group_rows, width = memory.shape
    asked = requests.shape[2]
    table_rows = n_node * asked
    events = shards * slots
    chunk = math.gcd(events, 512)
    turns = events // chunk
    chips = n_event // 2
    block = group_rows // n_event

    live = (jnp.arange(slots, dtype=jnp.int32)[None, :] < event_count[0][:, None]).astype(jnp.int32)
    parts = [event_source[0], event_partner[0], event_negative[0], event_time[0], live]
    parts.append(jnp.zeros((shards, LANES - 5 * slots), jnp.int32))
    packed = jnp.concatenate(parts, axis=1).reshape(shards, 1, LANES)

    vmem = pl.BlockSpec(memory_space=pltpu.VMEM)
    hbm = pl.BlockSpec(memory_space=pl.ANY)
    dma = pltpu.SemaphoreType.DMA
    return pl.pallas_call(
        functools.partial(kernel, n_node, n_event, chunk),
        out_shape=jax.ShapeDtypeStruct((block, width), F32),
        in_specs=[vmem, hbm, vmem, hbm, hbm, hbm, hbm, vmem, vmem],
        out_specs=vmem,
        scratch_shapes=[
            pltpu.VMEM(memory.shape, BF),
            pltpu.VMEM(w_input.shape, BF),
            pltpu.VMEM(w_state.shape, BF),
            pltpu.VMEM(w_pair.shape, BF),
            pltpu.VMEM((shards, slots, feat_width), BF),
            pltpu.VMEM((shards, 1, LANES), jnp.int32),
            pltpu.VMEM((n_node, 1, asked), jnp.int32),
            pltpu.VMEM((n_node, asked, width), BF),
            pltpu.VMEM((n_node, asked, width), BF),
            pltpu.VMEM((turns, chunk, 3 * width), F32),
            pltpu.VMEM((turns, chunk, width), F32),
            pltpu.VMEM((turns, chunk, width), BF),
            pltpu.VMEM((turns, 3, 8, chunk), jnp.int32),
            pltpu.VMEM((turns, 3, chunk, LANES), jnp.int32),
            pltpu.VMEM((table_rows, width), F32),
            pltpu.VMEM((turns, chunk, width), BF),
            pltpu.VMEM((turns, chunk, width), BF),
            pltpu.VMEM((n_node, asked, width), BF),
            pltpu.VMEM((n_node, asked, width), BF),
            pltpu.VMEM((asked, width), BF),
            pltpu.VMEM((n_event, block, width), F32),
            pltpu.VMEM((chips, block, width), F32),
            pltpu.VMEM((chips, block, width), F32),
            pltpu.VMEM((chips, block, width), BF),
            pltpu.VMEM((chips, block, width), BF),
            dma((4,)),
            dma,
            dma,
            dma,
            dma,
            dma((n_node,)),
            dma((n_node,)),
            dma((n_node,)),
            dma((n_node,)),
            dma((n_node,)),
            dma((n_node,)),
            dma((chips,)),
            dma((chips,)),
            dma((chips,)),
            dma((chips,)),
        ],
        compiler_params=pltpu.CompilerParams(
            collective_id=0, has_side_effects=True, vmem_limit_bytes=56 * 1024 * 1024
        ),
        name="memory_step",
    )(
        packed,
        event_feat[0],
        requests[0][:, None, :],
        memory,
        w_input,
        w_state,
        w_pair,
        gate_bias[None, :],
        time_freq[None, :],
    )


def solution(mesh):
    by_device = ("node", "event")
    in_specs = (
        P("node", None),
        P(by_device, None, None, None),
        P(by_device, None, None),
        P(by_device, None, None),
        P(by_device, None, None),
        P(by_device, None, None),
        P(by_device, None),
        P(by_device, None, None),
        P(),
        P(),
        P(),
        P(),
        P(),
    )
    out_specs = P(by_device, None)
    return jax.shard_map(local, mesh=mesh, in_specs=in_specs, out_specs=out_specs, check_vma=False)
```

```python
import functools
import math

import jax
import jax.numpy as jnp
from jax import lax
from jax.experimental import pallas as pl
from jax.experimental.pallas import tpu as pltpu
from jax.sharding import PartitionSpec as P

MESH = pl.DeviceIdType.MESH
BF = jnp.bfloat16
F32 = jnp.float32
LANES = 128
OUT = pltpu.VMEM


def mm(a, b):
    return jnp.dot(a, b, preferred_element_type=F32)


def mm_nt(a, b):
    return lax.dot_general(a, b, (((1,), (1,)), ((), ())), preferred_element_type=F32)


def split(value):
    high = value.astype(BF)
    return high, (value - high.astype(F32)).astype(BF)


def one_hot(mask):
    return jnp.where(mask, 1.0, 0.0).astype(BF)


def pick_matrix(column, total):
    lane = lax.broadcasted_iota(jnp.int32, column.shape, 1)
    return jnp.concatenate(
        [one_hot(column == lane + start) for start in range(0, total, LANES)], axis=1
    )


def spread_matrix(row, total, base):
    ids = lax.broadcasted_iota(jnp.int32, (total, row.shape[1]), 0) + base
    return one_hot(ids == row)


def kernel(
    n_node,
    n_event,
    chunk,
    ids_hbm,
    count_hbm,
    feat_ref,
    req_ref,
    mem_hbm,
    win_hbm,
    wst_hbm,
    wpair_hbm,
    bias_hbm,
    freq_hbm,
    out_ref,
    mem,
    win,
    wst,
    wpair,
    bias,
    freq,
    ids,
    count,
    stage,
    pack,
    feats,
    packs,
    wanted,
    wanted_pair,
    fetched,
    table,
    pre,
    recur,
    prev,
    ids_row,
    source_row,
    source_pair,
    live,
    pick,
    spread,
    place,
    table_grad,
    renew_grad,
    state_grad,
    cur,
    cur_pair,
    back_out,
    back_in,
    back_pair,
    acc,
    block_out,
    block_in,
    load_sem,
    feat_send,
    feat_recv,
    pack_send,
    pack_recv,
    req_send,
    req_recv,
    tab_send,
    tab_recv,
    list_send,
    list_recv,
    cur_send,
    cur_recv,
    back_send,
    back_recv,
    pass_send,
    pass_recv,
    block_send,
    block_recv,
):
    shards = n_node * n_event
    node, event = lax.axis_index("node"), lax.axis_index("event")
    me = node * n_event + event
    slots = feat_ref.shape[1]
    width = mem.shape[1]
    group_rows = mem.shape[0]
    asked = req_ref.shape[2]
    table_rows = n_node * asked
    events = shards * slots
    turns = events // chunk
    chips = n_event // 2
    chip, core = event // 2, event % 2
    sibling = event + 1 - 2 * core
    block = group_rows // n_event
    half = width // 2

    barrier = pltpu.get_barrier_semaphore()

    @pl.loop(1, shards)
    def _(k):
        peer = lax.rem(me + k, shards)
        pl.semaphore_signal(
            barrier, inc=1, device_id=(peer // n_event, peer % n_event), device_id_type=MESH
        )

    small = [
        pltpu.make_async_copy(ids_hbm[k], ids.at[k], load_sem.at[k]) for k in range(4)
    ] + [pltpu.make_async_copy(count_hbm, count, load_sem.at[4])]
    loads = [
        pltpu.make_async_copy(source, target, load_sem.at[5 + k])
        for k, (source, target) in enumerate(
            (
                (mem_hbm, mem),
                (win_hbm, win),
                (wst_hbm, wst),
                (wpair_hbm, wpair),
                (bias_hbm, bias),
                (freq_hbm, freq),
            )
        )
    ]
    own_list = pltpu.make_async_copy(req_ref.at[node], wanted.at[node], req_recv.at[node])
    own_feat = pltpu.make_async_copy(feat_ref.at[me], feats.at[me], feat_recv)
    for load in small + loads + [own_list, own_feat]:
        load.start()
    stage[...] = jnp.zeros_like(stage)
    for load in small:
        load.wait()
    for k in range(4):
        stage[k * slots : (k + 1) * slots, :shards] = ids[k]
    slot = lax.broadcasted_iota(jnp.int32, (slots, shards), 0)
    stage[4 * slots : 5 * slots, :shards] = jnp.where(slot < count[...], 1, 0)
    pack[...] = stage[...].T[:shards].reshape(shards, 1, LANES)
    packs[me] = pack[me]
    pl.semaphore_wait(barrier, shards - 1)

    def to_node(k):
        return lax.rem(node + k, n_node)

    def arrived(buffer, sem, slot):
        pltpu.make_async_copy(buffer.at[slot], buffer.at[slot], sem.at[slot]).wait()

    def request_copy(k):
        peer = to_node(k)
        return pltpu.make_async_remote_copy(
            src_ref=req_ref.at[peer],
            dst_ref=wanted.at[node],
            send_sem=req_send.at[peer],
            recv_sem=req_recv.at[node],
            device_id=(peer, event),
            device_id_type=MESH,
        )

    for k in range(n_node - 1, 0, -1):
        request_copy(k).start()

    @pl.loop(1, shards)
    def _(k):
        peer = lax.rem(me + k, shards)
        target = (peer // n_event, peer % n_event)
        pltpu.make_async_remote_copy(
            src_ref=pack.at[peer],
            dst_ref=packs.at[me],
            send_sem=pack_send,
            recv_sem=pack_recv,
            device_id=target,
            device_id_type=MESH,
        ).start()
        pltpu.make_async_remote_copy(
            src_ref=feat_ref.at[peer],
            dst_ref=feats.at[me],
            send_sem=feat_send,
            recv_sem=feat_recv,
            device_id=target,
            device_id_type=MESH,
        ).start()

    for k in range(n_node):
        arrived(wanted, req_recv, to_node(k))
    loads[0].wait()
    columns = [jnp.broadcast_to(wanted[g], (LANES, asked)).T for g in range(n_node)]
    picked = mm(pick_matrix(jnp.concatenate(columns, axis=0), group_rows), mem[...]).astype(BF)
    fetched[...] = picked.reshape(n_node, asked, width)

    def table_copy(k):
        peer = to_node(k)
        return pltpu.make_async_remote_copy(
            src_ref=fetched.at[peer],
            dst_ref=table.at[node],
            send_sem=tab_send.at[peer],
            recv_sem=tab_recv.at[node],
            device_id=(peer, event),
            device_id_type=MESH,
        )

    for k in range(n_node - 1, 0, -1):
        table_copy(k).start()
    table[node] = fetched[node]

    def to_sibling(source, target, send_sem, recv_sem):
        return pltpu.make_async_remote_copy(
            src_ref=source,
            dst_ref=target,
            send_sem=send_sem,
            recv_sem=recv_sem,
            device_id=(node, sibling),
            device_id_type=MESH,
        )

    wanted_copy = to_sibling(wanted, wanted_pair, list_send.at[0], list_recv.at[0])
    wanted_copy.start()

    pltpu.make_async_copy(feats, feats, feat_recv).wait()
    others = packs.at[pl.ds(0, shards - 1)]
    pltpu.make_async_copy(others, others, pack_recv).wait()
    for load in loads[1:]:
        load.wait()
    codes = packs[...].reshape(shards, LANES)
    code_parts = jnp.concatenate([codes >> 8, codes & 255], axis=1).astype(F32).astype(BF)
    kinds = 5
    from_lane = lax.broadcasted_iota(jnp.int32, (2 * LANES, kinds * LANES), 0)
    to_kind = lax.broadcasted_iota(jnp.int32, (2 * LANES, kinds * LANES), 1) // LANES
    weight = jnp.where(from_lane < LANES, 256.0, 1.0)
    gather_kind = jnp.where((from_lane % LANES) // slots == to_kind, weight, 0.0).astype(BF)
    bias_row = jnp.concatenate([bias[k : k + 1, :] for k in range(bias.shape[0])], axis=1)

    @pl.loop(0, turns)
    def _(t):
        first = t * (chunk // slots)
        home = lax.broadcasted_iota(jnp.int32, (chunk, shards), 0) // slots + first
        from_home = one_hot(home == lax.broadcasted_iota(jnp.int32, (chunk, shards), 1))
        mine = mm(from_home, code_parts)
        lane = lax.broadcasted_iota(jnp.int32, (chunk, 2 * LANES), 1)
        row = lax.broadcasted_iota(jnp.int32, (chunk, 2 * LANES), 0)
        mine = jnp.where(lane % slots == row % slots, mine, 0.0).astype(BF)
        columns = mm(mine, gather_kind)
        times = columns[:, 3 * LANES : 4 * LANES]
        live[t] = columns[:, 4 * LANES :]
        for kind in range(2):
            line = columns[:, (kind + 1) * LANES : (kind + 2) * LANES].T
            ids_row[t, kind] = line[:8].astype(jnp.int32)
        source_row[t] = columns[:, :LANES].T[:8].astype(jnp.int32)
        source = columns[:, :LANES].astype(jnp.int32)
        current = mm(pick_matrix(source, group_rows), mem[...]).astype(BF)
        from_state = mm(current, wst[...])
        timing = jnp.cos(times * freq[...]).astype(BF)
        feature = feats[pl.ds(first, chunk // slots)].reshape(chunk, feat_ref.shape[2])
        from_rest = mm(jnp.concatenate([feature, timing], axis=1), win[width:, :])
        prev[t] = current
        recur[t] = from_state[:, 2 * width :]
        gates = from_rest[:, : 2 * width] + from_state[:, : 2 * width]
        pre[t] = jnp.concatenate([gates, from_rest[:, 2 * width :]], axis=1) + bias_row
        for kind in range(2):
            column = columns[:, (kind + 1) * LANES : (kind + 2) * LANES].astype(jnp.int32)
            pick[t, kind * chunk : (kind + 1) * chunk] = pick_matrix(column, table_rows)
            spread[t, :, kind * chunk : (kind + 1) * chunk] = spread_matrix(
                ids_row[t, kind][:1], table_rows, 0
            )

    source_copy = to_sibling(source_row, source_pair, list_send.at[1], list_recv.at[1])
    source_copy.start()
    arrived_pair = pltpu.make_async_copy(wanted_pair, wanted_pair, list_recv.at[0])
    arrived_pair.wait()
    listed = jnp.concatenate(
        [wanted[g] for g in range(n_node)]
        + [wanted[node]]
        + [wanted_pair[g] for g in range(n_node)]
        + [wanted_pair[node]],
        axis=1,
    )

    @pl.loop(0, chips)
    def _(j):
        place[j] = spread_matrix(listed, block, (2 * j + core) * block)

    for k in range(1, n_node):
        arrived(table, tab_recv, to_node(k))
    table_grad[...] = jnp.zeros_like(table_grad)
    factor = 1.0 / math.sqrt(width)

    @pl.loop(0, turns)
    def _(t):
        rows = mm(pick[t], table[...].reshape(table_rows, width)).astype(BF)
        partner = rows[:chunk]
        valid = live[t][:, :1]
        all_pre = pre[t] + mm(partner, win[:width, :])
        recurrent = recur[t]
        previous = prev[t].astype(F32)
        reset = jax.nn.sigmoid(all_pre[:, :width])
        update = jax.nn.sigmoid(all_pre[:, width : 2 * width])
        candidate = jnp.tanh(all_pre[:, 2 * width :] + reset * recurrent)
        renewed = (1.0 - update) * candidate + update * previous
        keys = mm(rows, wpair[...])
        key_pos, key_neg = keys[:chunk], keys[chunk:]
        score_pos = jnp.sum(renewed * key_pos, axis=1, keepdims=True) * factor
        score_neg = jnp.sum(renewed * key_neg, axis=1, keepdims=True) * factor
        weight_pos = -valid * jax.nn.sigmoid(-score_pos)
        weight_neg = valid * jax.nn.sigmoid(score_neg)
        grad_renewed = (weight_pos * key_pos + weight_neg * key_neg) * factor
        grad_keypos = (weight_pos * renewed * factor).astype(BF)
        grad_keyneg = (weight_neg * renewed * factor).astype(BF)
        grad_cand = grad_renewed * (1.0 - update) * (1.0 - candidate * candidate)
        grad_reset = (grad_cand * recurrent * reset * (1.0 - reset)).astype(BF)
        grad_update = (
            grad_renewed * (previous - candidate) * update * (1.0 - update)
        ).astype(BF)
        input_back = jnp.concatenate([grad_reset, grad_update, grad_cand.astype(BF)], axis=1)
        renew_grad[t] = grad_renewed * update
        state_grad[t] = jnp.concatenate(
            [grad_reset, grad_update, (grad_cand * reset).astype(BF)], axis=1
        )
        grad_keys = mm_nt(jnp.concatenate([grad_keypos, grad_keyneg], axis=0), wpair[...])
        grad_partner = mm_nt(input_back, win[:width, :]) + grad_keys[:chunk]
        high, low = split(jnp.concatenate([grad_partner, grad_keys[chunk:]], axis=0))
        table_grad[...] += mm(spread[t], high) + mm(spread[t], low)

    high, low = split(table_grad[...])
    for h in range(2):
        back_out[h] = high[:, h * half : (h + 1) * half].reshape(n_node, asked, half)

    def back_copy(h, k):
        peer = to_node(k)
        return pltpu.make_async_remote_copy(
            src_ref=back_out.at[h, peer],
            dst_ref=back_in.at[h, node],
            send_sem=back_send.at[h, peer],
            recv_sem=back_recv.at[h, node],
            device_id=(peer, event),
            device_id_type=MESH,
        )

    def pass_copy(h, slot):
        return to_sibling(
            back_in.at[h, slot],
            back_pair.at[h, slot],
            pass_send.at[h, slot],
            pass_recv.at[h, slot],
        )

    for h in range(2):
        for k in range(n_node - 1, 0, -1):
            back_copy(h, k).start()
    table_grad[...] = low.astype(F32)
    own_low = table_grad[pl.ds(pl.multiple_of(node * asked, asked), asked), :].astype(BF)
    for h in range(2):
        back_in[h, node] = back_out[h, node]
        back_in[h, n_node] = own_low[:, h * half : (h + 1) * half]
        pass_copy(h, node).start()
        pass_copy(h, n_node).start()

    @pl.loop(0, turns)
    def _(t):
        high, low = split(renew_grad[t] + mm_nt(state_grad[t], wst[...]))
        cur[t, 0] = high
        cur[t, 1] = low

    cur_copy = to_sibling(cur, cur_pair, cur_send, cur_recv)
    cur_copy.start()

    @pl.loop(0, chips)
    def _(j):
        total = jnp.zeros((block, width), F32)
        for t in range(turns):
            at = spread_matrix(source_row[t][:1], block, (2 * j + core) * block)
            total += mm(at, cur[t, 0]) + mm(at, cur[t, 1])
        acc[j] = total

    pltpu.make_async_copy(source_pair, source_pair, list_recv.at[1]).wait()
    pltpu.make_async_copy(cur_pair, cur_pair, cur_recv).wait()

    @pl.loop(0, chips)
    def _(j):
        total = acc[j]
        for t in range(turns):
            at = spread_matrix(source_pair[t][:1], block, (2 * j + core) * block)
            total += mm(at, cur_pair[t, 0]) + mm(at, cur_pair[t, 1])
        acc[j] = total

    def block_copy(h, j):
        return pltpu.make_async_remote_copy(
            src_ref=block_out.at[h, j],
            dst_ref=block_in.at[h, chip],
            send_sem=block_send.at[h, j],
            recv_sem=block_recv.at[h, chip],
            device_id=(node, 2 * j + core),
            device_id_type=MESH,
        )

    own = []
    for h in range(2):
        for k in range(1, n_node):
            slot = to_node(k)
            arrived(back_in.at[h], back_recv.at[h], slot)
            pass_copy(h, slot).start()
        for slot in range(n_node + 1):
            arrived(back_pair.at[h], pass_recv.at[h], slot)
        rows = (n_node + 1) * asked
        returned = jnp.concatenate(
            [back_in[h].reshape(rows, half), back_pair[h].reshape(rows, half)], axis=0
        )

        def whole_block(j):
            return acc[j][:, h * half : (h + 1) * half] + mm(place[j], returned)

        @pl.loop(1, chips)
        def _(k):
            j = lax.rem(chip + k, chips)
            block_out[h, j] = whole_block(j).astype(BF)
            block_copy(h, j).start()

        own.append(whole_block(chip))

    for h in range(2):
        total = own[h]
        for k in range(1, chips):
            j = lax.rem(chip + k, chips)
            arrived(block_in.at[h], block_recv.at[h], j)
            total += block_in[h, j].astype(F32)
        out_ref[:, h * half : (h + 1) * half] = total

    for k in range(1, n_node):
        request_copy(k).wait_send()
        table_copy(k).wait_send()
    for h in range(2):
        for k in range(1, n_node):
            back_copy(h, k).wait_send()
        for slot in range(n_node + 1):
            pass_copy(h, slot).wait_send()
        for k in range(1, chips):
            block_copy(h, lax.rem(chip + k, chips)).wait_send()
    wanted_copy.wait_send()
    source_copy.wait_send()
    cur_copy.wait_send()
    sent = feats.at[pl.ds(0, shards - 1)]
    pltpu.make_async_copy(sent, sent, feat_send).wait()
    pltpu.make_async_copy(others, others, pack_send).wait()


def local(
    memory,
    event_feat,
    event_source,
    event_partner,
    event_negative,
    event_time,
    event_count,
    requests,
    w_input,
    w_state,
    w_pair,
    gate_bias,
    time_freq,
):
    n_node = lax.axis_size("node")
    n_event = lax.axis_size("event")
    shards = n_node * n_event
    slots, feat_width = event_feat.shape[2:]
    group_rows, width = memory.shape
    asked = requests.shape[2]
    table_rows = n_node * asked
    events = shards * slots
    chunk = math.gcd(events, 512)
    turns = events // chunk
    chips = n_event // 2
    block = group_rows // n_event
    half = width // 2
    listed = (n_node + 1) * asked
    bias_rows = gate_bias.shape[0] // LANES

    vmem = pl.BlockSpec(memory_space=pltpu.VMEM)
    hbm = pl.BlockSpec(memory_space=pl.ANY)
    dma = pltpu.SemaphoreType.DMA
    ids = [value[0].T for value in (event_source, event_partner, event_negative, event_time)]
    return pl.pallas_call(
        functools.partial(kernel, n_node, n_event, chunk),
        out_shape=OUT((block, width), F32),
        in_specs=[[hbm] * 4] + [hbm] * 9,
        out_specs=vmem,
        scratch_shapes=[
            pltpu.VMEM(memory.shape, BF),
            pltpu.VMEM(w_input.shape, BF),
            pltpu.VMEM(w_state.shape, BF),
            pltpu.VMEM(w_pair.shape, BF),
            pltpu.VMEM((bias_rows, LANES), F32),
            pltpu.VMEM((1, LANES), F32),
            pltpu.VMEM((4, slots, shards), jnp.int32),
            pltpu.VMEM((1, shards), jnp.int32),
            pltpu.VMEM((LANES, max(shards, LANES)), jnp.int32),
            pltpu.VMEM((shards, 1, LANES), jnp.int32),
            pltpu.VMEM((shards, slots, feat_width), BF),
            pltpu.VMEM((shards, 1, LANES), jnp.int32),
            pltpu.VMEM((n_node, 1, asked), jnp.int32),
            pltpu.VMEM((n_node, 1, asked), jnp.int32),
            pltpu.VMEM((n_node, asked, width), BF),
            pltpu.VMEM((n_node, asked, width), BF),
            pltpu.VMEM((turns, chunk, 3 * width), F32),
            pltpu.VMEM((turns, chunk, width), F32),
            pltpu.VMEM((turns, chunk, width), BF),
            pltpu.VMEM((turns, 2, 8, chunk), jnp.int32),
            pltpu.VMEM((turns, 8, chunk), jnp.int32),
            pltpu.VMEM((turns, 8, chunk), jnp.int32),
            pltpu.VMEM((turns, chunk, LANES), F32),
            pltpu.VMEM((turns, 2 * chunk, table_rows), BF),
            pltpu.VMEM((turns, table_rows, 2 * chunk), BF),
            pltpu.VMEM((chips, block, 2 * listed), BF),
            pltpu.VMEM((table_rows, width), F32),
            pltpu.VMEM((turns, chunk, width), F32),
            pltpu.VMEM((turns, chunk, 3 * width), BF),
            pltpu.VMEM((turns, 2, chunk, width), BF),
            pltpu.VMEM((turns, 2, chunk, width), BF),
            pltpu.VMEM((2, n_node, asked, half), BF),
            pltpu.VMEM((2, n_node + 1, asked, half), BF),
            pltpu.VMEM((2, n_node + 1, asked, half), BF),
            pltpu.VMEM((chips, block, width), F32),
            pltpu.VMEM((2, chips, block, half), BF),
            pltpu.VMEM((2, chips, block, half), BF),
            dma((11,)),
            dma,
            dma,
            dma,
            dma,
            dma((n_node,)),
            dma((n_node,)),
            dma((n_node,)),
            dma((n_node,)),
            dma((2,)),
            dma((2,)),
            dma,
            dma,
            dma((2, n_node)),
            dma((2, n_node)),
            dma((2, n_node + 1)),
            dma((2, n_node + 1)),
            dma((2, chips)),
            dma((2, chips)),
        ],
        compiler_params=pltpu.CompilerParams(
            collective_id=0, has_side_effects=True, vmem_limit_bytes=60 * 1024 * 1024
        ),
        name="memory_step",
    )(
        ids,
        event_count,
        event_feat[0],
        requests[0][:, None, :],
        memory,
        w_input,
        w_state,
        w_pair,
        gate_bias.reshape(bias_rows, LANES),
        time_freq[None, :],
    )


def solution(mesh):
    by_device = ("node", "event")
    in_specs = (
        P("node", None),
        P(by_device, None, None, None),
        P(by_device, None, None),
        P(by_device, None, None),
        P(by_device, None, None),
        P(by_device, None, None),
        P(by_device, None),
        P(by_device, None, None),
        P(),
        P(),
        P(),
        P(),
        P(),
    )
    out_specs = P(by_device, None)
    return jax.shard_map(local, mesh=mesh, in_specs=in_specs, out_specs=out_specs, check_vma=False)
```

```python
import functools
import math

import jax
import jax.numpy as jnp
from jax import lax
from jax.experimental import pallas as pl
from jax.experimental.pallas import tpu as pltpu
from jax.sharding import PartitionSpec as P

MESH = pl.DeviceIdType.MESH
BF = jnp.bfloat16
F32 = jnp.float32
LANES = 128
OUT = pltpu.VMEM


def mm(a, b):
    return jnp.dot(a, b, preferred_element_type=F32)


def mm_nt(a, b):
    return lax.dot_general(a, b, (((1,), (1,)), ((), ())), preferred_element_type=F32)


def split(value):
    high = value.astype(BF)
    return high, (value - high.astype(F32)).astype(BF)


def one_hot(mask):
    return jnp.where(mask, 1.0, 0.0).astype(BF)


def pick_matrix(column, total):
    lane = lax.broadcasted_iota(jnp.int32, column.shape, 1)
    return jnp.concatenate(
        [one_hot(column == lane + start) for start in range(0, total, LANES)], axis=1
    )


def spread_matrix(row, total, base):
    ids = lax.broadcasted_iota(jnp.int32, (total, row.shape[1]), 0) + base
    return one_hot(ids == row)


def sigmoid(value):
    return 0.5 * jnp.tanh(0.5 * value) + 0.5


def cosine(value):
    turns = jnp.floor(value * (1.0 / math.pi) + 0.5)
    rest = (value - turns * 3.140625) - turns * (math.pi - 3.140625)
    square = rest * rest
    series = jnp.full_like(value, 1.0 / math.factorial(12))
    for power in range(10, -1, -2):
        sign = 1.0 if power % 4 == 0 else -1.0
        series = series * square + sign / math.factorial(power)
    odd = turns - 2.0 * jnp.floor(0.5 * turns)
    return series * (1.0 - 2.0 * odd)


def kernel(
    n_node,
    n_event,
    chunk,
    ids_hbm,
    count_hbm,
    feat_ref,
    req_ref,
    mem_hbm,
    win_hbm,
    wst_hbm,
    wpair_hbm,
    bias_hbm,
    freq_hbm,
    out_ref,
    mem,
    win,
    wst,
    wpair,
    bias,
    freq,
    ids,
    count,
    stage,
    pack,
    feats_relay,
    packs_relay,
    feats,
    packs,
    wanted,
    wanted_pair,
    fetched,
    table,
    pre,
    recur,
    prev,
    ids_row,
    source_row,
    source_pair,
    live,
    pick,
    spread,
    place_own,
    place,
    table_grad,
    renew_grad,
    state_grad,
    cur,
    cur_pair,
    back_out,
    back_in,
    back_pair,
    acc,
    block_out,
    block_in,
    load_sem,
    feat_send,
    feat_recv,
    pack_send,
    pack_recv,
    feat_out,
    feat_in,
    pack_out,
    pack_in,
    req_send,
    req_recv,
    tab_send,
    tab_recv,
    list_send,
    list_recv,
    cur_send,
    cur_recv,
    back_send,
    back_recv,
    pass_send,
    pass_recv,
    block_send,
    block_recv,
):
    shards = n_node * n_event
    node, event = lax.axis_index("node"), lax.axis_index("event")
    slots = feat_ref.shape[1]
    width = mem.shape[1]
    group_rows = mem.shape[0]
    asked = req_ref.shape[2]
    table_rows = n_node * asked
    events = shards * slots
    turns = events // chunk
    chips = n_event // 2
    chip, core = event // 2, event % 2
    sibling = event + 1 - 2 * core
    block = group_rows // n_event
    half = width // 2

    barrier = pltpu.get_barrier_semaphore()

    def to_node(k):
        return lax.rem(node + k, n_node)

    def to_event(k):
        return lax.rem(event + k, n_event)

    for k in range(1, n_node):
        pl.semaphore_signal(barrier, inc=1, device_id=(to_node(k), event), device_id_type=MESH)

    @pl.loop(1, n_event)
    def _(k):
        pl.semaphore_signal(barrier, inc=1, device_id=(node, to_event(k)), device_id_type=MESH)

    small = [
        pltpu.make_async_copy(ids_hbm[k], ids.at[k], load_sem.at[k]) for k in range(4)
    ] + [pltpu.make_async_copy(count_hbm, count, load_sem.at[4])]
    loads = [
        pltpu.make_async_copy(source, target, load_sem.at[5 + k])
        for k, (source, target) in enumerate(
            (
                (mem_hbm, mem),
                (win_hbm, win),
                (wst_hbm, wst),
                (wpair_hbm, wpair),
                (bias_hbm, bias),
                (freq_hbm, freq),
            )
        )
    ]
    own_list = pltpu.make_async_copy(req_ref.at[node], wanted.at[node], req_recv.at[node])
    own_feat = pltpu.make_async_copy(
        feat_ref.at[pl.ds(node * n_event, n_event)], feats_relay.at[node], feat_recv.at[node]
    )
    for load in small + loads + [own_list, own_feat]:
        load.start()
    stage[...] = jnp.zeros_like(stage)
    for load in small:
        load.wait()
    for k in range(4):
        stage[k * slots : (k + 1) * slots, :shards] = ids[k]
    slot = lax.broadcasted_iota(jnp.int32, (slots, shards), 0)
    stage[4 * slots : 5 * slots, :shards] = jnp.where(slot < count[...], 1, 0)
    pack[...] = stage[...].T[:shards].reshape(shards, 1, LANES)
    packs_relay[node] = pack[pl.ds(node * n_event, n_event)]
    pl.semaphore_wait(barrier, n_node + n_event - 2)

    def arrived(buffer, sem, slot):
        pltpu.make_async_copy(buffer.at[slot], buffer.at[slot], sem.at[slot]).wait()

    def request_copy(k):
        peer = to_node(k)
        return pltpu.make_async_remote_copy(
            src_ref=req_ref.at[peer],
            dst_ref=wanted.at[node],
            send_sem=req_send.at[peer],
            recv_sem=req_recv.at[node],
            device_id=(peer, event),
            device_id_type=MESH,
        )

    for k in range(n_node - 1, 0, -1):
        request_copy(k).start()

    def to_group(k, source, target, send_sem, recv_sem):
        peer = to_node(k)
        return pltpu.make_async_remote_copy(
            src_ref=source.at[pl.ds(peer * n_event, n_event)],
            dst_ref=target.at[node],
            send_sem=send_sem.at[peer],
            recv_sem=recv_sem.at[node],
            device_id=(peer, event),
            device_id_type=MESH,
        )

    def group_copies(k):
        return (
            to_group(k, pack, packs_relay, pack_send, pack_recv),
            to_group(k, feat_ref, feats_relay, feat_send, feat_recv),
        )

    for k in range(n_node - 1, 0, -1):
        for copy in group_copies(k):
            copy.start()

    for k in range(n_node):
        arrived(wanted, req_recv, to_node(k))
    loads[0].wait()
    columns = [jnp.broadcast_to(wanted[g], (LANES, asked)).T for g in range(n_node)]
    picked = mm(pick_matrix(jnp.concatenate(columns, axis=0), group_rows), mem[...]).astype(BF)
    fetched[...] = picked.reshape(n_node, asked, width)

    def table_copy(k):
        peer = to_node(k)
        return pltpu.make_async_remote_copy(
            src_ref=fetched.at[peer],
            dst_ref=table.at[node],
            send_sem=tab_send.at[peer],
            recv_sem=tab_recv.at[node],
            device_id=(peer, event),
            device_id_type=MESH,
        )

    for k in range(n_node - 1, 0, -1):
        table_copy(k).start()
    table[node] = fetched[node]

    def to_sibling(source, target, send_sem, recv_sem):
        return pltpu.make_async_remote_copy(
            src_ref=source,
            dst_ref=target,
            send_sem=send_sem,
            recv_sem=recv_sem,
            device_id=(node, sibling),
            device_id_type=MESH,
        )

    wanted_copy = to_sibling(wanted, wanted_pair, list_send.at[0], list_recv.at[0])
    wanted_copy.start()

    def to_owner(k, source, target, send_sem, recv_sem):
        peer = to_event(k)
        return pltpu.make_async_remote_copy(
            src_ref=source.at[:, peer],
            dst_ref=target.at[:, event],
            send_sem=send_sem.at[peer],
            recv_sem=recv_sem.at[event],
            device_id=(node, peer),
            device_id_type=MESH,
        )

    def owner_copies(k):
        return (
            to_owner(k, packs_relay, packs, pack_out, pack_in),
            to_owner(k, feats_relay, feats, feat_out, feat_in),
        )

    for k in range(n_node):
        if k > 0:
            arrived(packs_relay, pack_recv, to_node(k))
        arrived(feats_relay, feat_recv, to_node(k))

    @pl.loop(1, n_event)
    def _(k):
        for copy in owner_copies(k):
            copy.start()

    kept = [
        pltpu.make_async_copy(packs_relay.at[:, event], packs.at[:, event], pack_in.at[event]),
        pltpu.make_async_copy(feats_relay.at[:, event], feats.at[:, event], feat_in.at[event]),
    ]
    for copy in kept:
        copy.start()

    for load in loads[1:]:
        load.wait()

    @pl.loop(0, n_event)
    def _(e):
        for buffer, sem in ((packs, pack_in), (feats, feat_in)):
            pltpu.make_async_copy(buffer.at[:, e], buffer.at[:, e], sem.at[e]).wait()

    codes = packs[...].reshape(shards, LANES)
    code_parts = jnp.concatenate([codes >> 8, codes & 255], axis=1).astype(F32).astype(BF)
    kinds = 5
    from_lane = lax.broadcasted_iota(jnp.int32, (2 * LANES, kinds * LANES), 0)
    to_kind = lax.broadcasted_iota(jnp.int32, (2 * LANES, kinds * LANES), 1) // LANES
    weight = jnp.where(from_lane < LANES, 256.0, 1.0)
    gather_kind = jnp.where((from_lane % LANES) // slots == to_kind, weight, 0.0).astype(BF)
    bias_row = jnp.concatenate([bias[k : k + 1, :] for k in range(bias.shape[0])], axis=1)

    @pl.loop(0, turns)
    def _(t):
        first = t * (chunk // slots)
        home = lax.broadcasted_iota(jnp.int32, (chunk, shards), 0) // slots + first
        from_home = one_hot(home == lax.broadcasted_iota(jnp.int32, (chunk, shards), 1))
        mine = mm(from_home, code_parts)
        lane = lax.broadcasted_iota(jnp.int32, (chunk, 2 * LANES), 1)
        row = lax.broadcasted_iota(jnp.int32, (chunk, 2 * LANES), 0)
        mine = jnp.where(lane % slots == row % slots, mine, 0.0).astype(BF)
        columns = mm(mine, gather_kind)
        times = columns[:, 3 * LANES : 4 * LANES]
        live[t] = columns[:, 4 * LANES :]
        for kind in range(2):
            line = columns[:, (kind + 1) * LANES : (kind + 2) * LANES].T
            ids_row[t, kind] = line[:8].astype(jnp.int32)
        source_row[t] = columns[:, :LANES].T[:8].astype(jnp.int32)
        source = columns[:, :LANES].astype(jnp.int32)
        current = mm(pick_matrix(source, group_rows), mem[...]).astype(BF)
        from_state = mm(current, wst[...])
        timing = cosine(times * freq[...]).astype(BF)
        groups = chunk // (slots * n_event)
        feature = feats[pl.ds(t * groups, groups)].reshape(chunk, feat_ref.shape[2])
        from_rest = mm(jnp.concatenate([feature, timing], axis=1), win[width:, :])
        prev[t] = current
        recur[t] = from_state[:, 2 * width :]
        gates = from_rest[:, : 2 * width] + from_state[:, : 2 * width]
        pre[t] = jnp.concatenate([gates, from_rest[:, 2 * width :]], axis=1) + bias_row
        for kind in range(2):
            column = columns[:, (kind + 1) * LANES : (kind + 2) * LANES].astype(jnp.int32)
            pick[t, kind * chunk : (kind + 1) * chunk] = pick_matrix(column, table_rows)
            spread[t, :, kind * chunk : (kind + 1) * chunk] = spread_matrix(
                ids_row[t, kind][:1], table_rows, 0
            )

    source_copy = to_sibling(source_row, source_pair, list_send.at[1], list_recv.at[1])
    source_copy.start()
    arrived_pair = pltpu.make_async_copy(wanted_pair, wanted_pair, list_recv.at[0])
    arrived_pair.wait()
    listed_own = jnp.concatenate([wanted[node]] * 2 + [wanted_pair[node]] * 2, axis=1)
    listed = jnp.concatenate(
        [wanted[to_node(k)] for k in range(1, n_node)]
        + [wanted_pair[to_node(k)] for k in range(1, n_node)],
        axis=1,
    )

    @pl.loop(0, chips)
    def _(j):
        base = (2 * j + core) * block
        place_own[j] = spread_matrix(listed_own, block, base)
        place[j] = spread_matrix(listed, block, base)

    for k in range(1, n_node):
        arrived(table, tab_recv, to_node(k))
    table_grad[...] = jnp.zeros_like(table_grad)
    factor = 1.0 / math.sqrt(width)

    @pl.loop(0, turns)
    def _(t):
        rows = mm(pick[t], table[...].reshape(table_rows, width)).astype(BF)
        partner = rows[:chunk]
        valid = live[t][:, :1]
        all_pre = pre[t] + mm(partner, win[:width, :])
        recurrent = recur[t]
        previous = prev[t].astype(F32)
        reset = sigmoid(all_pre[:, :width])
        update = sigmoid(all_pre[:, width : 2 * width])
        candidate = jnp.tanh(all_pre[:, 2 * width :] + reset * recurrent)
        renewed = (1.0 - update) * candidate + update * previous
        keys = mm(rows, wpair[...])
        key_pos, key_neg = keys[:chunk], keys[chunk:]
        score_pos = jnp.sum(renewed * key_pos, axis=1, keepdims=True) * factor
        score_neg = jnp.sum(renewed * key_neg, axis=1, keepdims=True) * factor
        weight_pos = -valid * jax.nn.sigmoid(-score_pos)
        weight_neg = valid * jax.nn.sigmoid(score_neg)
        grad_renewed = (weight_pos * key_pos + weight_neg * key_neg) * factor
        grad_keypos = (weight_pos * renewed * factor).astype(BF)
        grad_keyneg = (weight_neg * renewed * factor).astype(BF)
        grad_cand = grad_renewed * (1.0 - update) * (1.0 - candidate * candidate)
        grad_reset = (grad_cand * recurrent * reset * (1.0 - reset)).astype(BF)
        grad_update = (
            grad_renewed * (previous - candidate) * update * (1.0 - update)
        ).astype(BF)
        input_back = jnp.concatenate([grad_reset, grad_update, grad_cand.astype(BF)], axis=1)
        renew_grad[t] = grad_renewed * update
        state_grad[t] = jnp.concatenate(
            [grad_reset, grad_update, (grad_cand * reset).astype(BF)], axis=1
        )
        grad_keys = mm_nt(jnp.concatenate([grad_keypos, grad_keyneg], axis=0), wpair[...])
        grad_partner = mm_nt(input_back, win[:width, :]) + grad_keys[:chunk]
        high, low = split(jnp.concatenate([grad_partner, grad_keys[chunk:]], axis=0))
        table_grad[...] += mm(spread[t], high) + mm(spread[t], low)

    high, low = split(table_grad[...])
    for h in range(2):
        back_out[h] = high[:, h * half : (h + 1) * half].reshape(n_node, asked, half)

    def back_copy(h, k):
        peer = to_node(k)
        return pltpu.make_async_remote_copy(
            src_ref=back_out.at[h, peer],
            dst_ref=back_in.at[h, node],
            send_sem=back_send.at[h, peer],
            recv_sem=back_recv.at[h, node],
            device_id=(peer, event),
            device_id_type=MESH,
        )

    def pass_copy(h, slot):
        return to_sibling(
            back_in.at[h, slot],
            back_pair.at[h, slot],
            pass_send.at[h, slot],
            pass_recv.at[h, slot],
        )

    for h in range(2):
        for k in range(n_node - 1, 0, -1):
            back_copy(h, k).start()
    table_grad[...] = low.astype(F32)
    own_low = table_grad[pl.ds(pl.multiple_of(node * asked, asked), asked), :].astype(BF)
    for h in range(2):
        back_in[h, node] = back_out[h, node]
        back_in[h, n_node] = own_low[:, h * half : (h + 1) * half]
        pass_copy(h, node).start()
        pass_copy(h, n_node).start()

    @pl.loop(0, turns)
    def _(t):
        high, low = split(renew_grad[t] + mm_nt(state_grad[t], wst[...]))
        cur[t, 0] = high
        cur[t, 1] = low

    cur_copy = to_sibling(cur, cur_pair, cur_send, cur_recv)
    cur_copy.start()

    @pl.loop(0, chips)
    def _(j):
        total = jnp.zeros((block, width), F32)
        for t in range(turns):
            at = spread_matrix(source_row[t][:1], block, (2 * j + core) * block)
            total += mm(at, cur[t, 0]) + mm(at, cur[t, 1])
        acc[j] = total

    for h in range(2):
        arrived(back_pair.at[h], pass_recv.at[h], node)
        arrived(back_pair.at[h], pass_recv.at[h], n_node)
    own_rows = jnp.concatenate(
        [
            jnp.concatenate([held[0, at], held[1, at]], axis=1)
            for held in (back_in, back_pair)
            for at in (node, n_node)
        ],
        axis=0,
    )
    pltpu.make_async_copy(source_pair, source_pair, list_recv.at[1]).wait()
    pltpu.make_async_copy(cur_pair, cur_pair, cur_recv).wait()

    @pl.loop(0, chips)
    def _(j):
        total = acc[j] + mm(place_own[j], own_rows)
        for t in range(turns):
            at = spread_matrix(source_pair[t][:1], block, (2 * j + core) * block)
            total += mm(at, cur_pair[t, 0]) + mm(at, cur_pair[t, 1])
        acc[j] = total

    def block_copy(h, j):
        return pltpu.make_async_remote_copy(
            src_ref=block_out.at[h, j],
            dst_ref=block_in.at[h, chip],
            send_sem=block_send.at[h, j],
            recv_sem=block_recv.at[h, chip],
            device_id=(node, 2 * j + core),
            device_id_type=MESH,
        )

    own = []
    for h in range(2):
        for k in range(1, n_node):
            slot = to_node(k)
            arrived(back_in.at[h], back_recv.at[h], slot)
            pass_copy(h, slot).start()
        for k in range(1, n_node):
            arrived(back_pair.at[h], pass_recv.at[h], to_node(k))
        returned = jnp.concatenate(
            [held[h, to_node(k)] for held in (back_in, back_pair) for k in range(1, n_node)],
            axis=0,
        )

        def whole_block(j):
            return acc[j][:, h * half : (h + 1) * half] + mm(place[j], returned)

        @pl.loop(1, chips)
        def _(k):
            j = lax.rem(chip + k, chips)
            block_out[h, j] = whole_block(j).astype(BF)
            block_copy(h, j).start()

        own.append(whole_block(chip))

    for h in range(2):
        total = own[h]
        for k in range(1, chips):
            j = lax.rem(chip + k, chips)
            arrived(block_in.at[h], block_recv.at[h], j)
            total += block_in[h, j].astype(F32)
        out_ref[:, h * half : (h + 1) * half] = total

    for k in range(1, n_node):
        request_copy(k).wait_send()
        table_copy(k).wait_send()
    for h in range(2):
        for k in range(1, n_node):
            back_copy(h, k).wait_send()
        for slot in range(n_node + 1):
            pass_copy(h, slot).wait_send()
        for k in range(1, chips):
            block_copy(h, lax.rem(chip + k, chips)).wait_send()
    wanted_copy.wait_send()
    source_copy.wait_send()
    cur_copy.wait_send()
    for k in range(1, n_node):
        for copy in group_copies(k):
            copy.wait_send()

    @pl.loop(1, n_event)
    def _(k):
        for copy in owner_copies(k):
            copy.wait_send()


def local(
    memory,
    event_feat,
    event_source,
    event_partner,
    event_negative,
    event_time,
    event_count,
    requests,
    w_input,
    w_state,
    w_pair,
    gate_bias,
    time_freq,
):
    n_node = lax.axis_size("node")
    n_event = lax.axis_size("event")
    shards = n_node * n_event
    slots, feat_width = event_feat.shape[2:]
    group_rows, width = memory.shape
    asked = requests.shape[2]
    table_rows = n_node * asked
    events = shards * slots
    chunk = math.gcd(events, 512)
    turns = events // chunk
    chips = n_event // 2
    block = group_rows // n_event
    half = width // 2
    listed = (n_node - 1) * asked
    bias_rows = gate_bias.shape[0] // LANES

    vmem = pl.BlockSpec(memory_space=pltpu.VMEM)
    hbm = pl.BlockSpec(memory_space=pl.ANY)
    dma = pltpu.SemaphoreType.DMA
    ids = [value[0].T for value in (event_source, event_partner, event_negative, event_time)]
    return pl.pallas_call(
        functools.partial(kernel, n_node, n_event, chunk),
        out_shape=OUT((block, width), F32),
        in_specs=[[hbm] * 4] + [hbm] * 9,
        out_specs=vmem,
        scratch_shapes=[
            pltpu.VMEM(memory.shape, BF),
            pltpu.VMEM(w_input.shape, BF),
            pltpu.VMEM(w_state.shape, BF),
            pltpu.VMEM(w_pair.shape, BF),
            pltpu.VMEM((bias_rows, LANES), F32),
            pltpu.VMEM((1, LANES), F32),
            pltpu.VMEM((4, slots, shards), jnp.int32),
            pltpu.VMEM((1, shards), jnp.int32),
            pltpu.VMEM((LANES, max(shards, LANES)), jnp.int32),
            pltpu.VMEM((shards, 1, LANES), jnp.int32),
            pltpu.VMEM((n_node, n_event, slots, feat_width), BF),
            pltpu.VMEM((n_node, n_event, 1, LANES), jnp.int32),
            pltpu.VMEM((n_node, n_event, slots, feat_width), BF),
            pltpu.VMEM((n_node, n_event, 1, LANES), jnp.int32),
            pltpu.VMEM((n_node, 1, asked), jnp.int32),
            pltpu.VMEM((n_node, 1, asked), jnp.int32),
            pltpu.VMEM((n_node, asked, width), BF),
            pltpu.VMEM((n_node, asked, width), BF),
            pltpu.VMEM((turns, chunk, 3 * width), F32),
            pltpu.VMEM((turns, chunk, width), F32),
            pltpu.VMEM((turns, chunk, width), BF),
            pltpu.VMEM((turns, 2, 8, chunk), jnp.int32),
            pltpu.VMEM((turns, 8, chunk), jnp.int32),
            pltpu.VMEM((turns, 8, chunk), jnp.int32),
            pltpu.VMEM((turns, chunk, LANES), F32),
            pltpu.VMEM((turns, 2 * chunk, table_rows), BF),
            pltpu.VMEM((turns, table_rows, 2 * chunk), BF),
            pltpu.VMEM((chips, block, 4 * asked), BF),
            pltpu.VMEM((chips, block, 2 * listed), BF),
            pltpu.VMEM((table_rows, width), F32),
            pltpu.VMEM((turns, chunk, width), F32),
            pltpu.VMEM((turns, chunk, 3 * width), BF),
            pltpu.VMEM((turns, 2, chunk, width), BF),
            pltpu.VMEM((turns, 2, chunk, width), BF),
            pltpu.VMEM((2, n_node, asked, half), BF),
            pltpu.VMEM((2, n_node + 1, asked, half), BF),
            pltpu.VMEM((2, n_node + 1, asked, half), BF),
            pltpu.VMEM((chips, block, width), F32),
            pltpu.VMEM((2, chips, block, half), BF),
            pltpu.VMEM((2, chips, block, half), BF),
            dma((11,)),
            dma((n_node,)),
            dma((n_node,)),
            dma((n_node,)),
            dma((n_node,)),
            dma((n_event,)),
            dma((n_event,)),
            dma((n_event,)),
            dma((n_event,)),
            dma((n_node,)),
            dma((n_node,)),
            dma((n_node,)),
            dma((n_node,)),
            dma((2,)),
            dma((2,)),
            dma,
            dma,
            dma((2, n_node)),
            dma((2, n_node)),
            dma((2, n_node + 1)),
            dma((2, n_node + 1)),
            dma((2, chips)),
            dma((2, chips)),
        ],
        compiler_params=pltpu.CompilerParams(
            collective_id=0, has_side_effects=True, vmem_limit_bytes=60 * 1024 * 1024
        ),
        name="memory_step",
    )(
        ids,
        event_count,
        event_feat[0],
        requests[0][:, None, :],
        memory,
        w_input,
        w_state,
        w_pair,
        gate_bias.reshape(bias_rows, LANES),
        time_freq[None, :],
    )


def solution(mesh):
    by_device = ("node", "event")
    in_specs = (
        P("node", None),
        P(by_device, None, None, None),
        P(by_device, None, None),
        P(by_device, None, None),
        P(by_device, None, None),
        P(by_device, None, None),
        P(by_device, None),
        P(by_device, None, None),
        P(),
        P(),
        P(),
        P(),
        P(),
    )
    out_specs = P(by_device, None)
    return jax.shard_map(local, mesh=mesh, in_specs=in_specs, out_specs=out_specs, check_vma=False)
```

```python
import functools
import math

import jax
import jax.numpy as jnp
from jax import lax
from jax.experimental import pallas as pl
from jax.experimental.pallas import tpu as pltpu
from jax.sharding import PartitionSpec as P

MESH = pl.DeviceIdType.MESH
BF = jnp.bfloat16
F32 = jnp.float32
LANES = 128
OUT = pltpu.VMEM


def mm(a, b):
    return jnp.dot(a, b, preferred_element_type=F32)


def mm_nt(a, b):
    return lax.dot_general(a, b, (((1,), (1,)), ((), ())), preferred_element_type=F32)


def split(value):
    high = value.astype(BF)
    return high, (value - high.astype(F32)).astype(BF)


def one_hot(mask):
    return jnp.where(mask, 1.0, 0.0).astype(BF)


def pick_matrix(column, total):
    lane = lax.broadcasted_iota(jnp.int32, column.shape, 1)
    return jnp.concatenate(
        [one_hot(column == lane + start) for start in range(0, total, LANES)], axis=1
    )


def spread_matrix(row, total, base):
    ids = lax.broadcasted_iota(jnp.int32, (total, row.shape[1]), 0) + base
    return one_hot(ids == row)


def sigmoid(value):
    return 0.5 * jnp.tanh(0.5 * value) + 0.5


def cosine(value):
    turns = jnp.floor(value * (1.0 / math.pi) + 0.5)
    rest = (value - turns * 3.140625) - turns * (math.pi - 3.140625)
    square = rest * rest
    series = jnp.full_like(value, 1.0 / math.factorial(12))
    for power in range(10, -1, -2):
        sign = 1.0 if power % 4 == 0 else -1.0
        series = series * square + sign / math.factorial(power)
    odd = turns - 2.0 * jnp.floor(0.5 * turns)
    return series * (1.0 - 2.0 * odd)


def kernel(
    n_node,
    n_event,
    chunk,
    ids_hbm,
    count_hbm,
    feat_ref,
    req_ref,
    mem_hbm,
    win_hbm,
    wst_hbm,
    wpair_hbm,
    bias_hbm,
    freq_hbm,
    out_ref,
    mem,
    win,
    wst,
    wpair,
    bias,
    freq,
    ids,
    count,
    stage,
    pack,
    feats_relay,
    packs_relay,
    feats,
    packs,
    wanted,
    wanted_pair,
    fetched,
    table,
    pre,
    recur,
    prev,
    ids_row,
    source_row,
    source_pair,
    live,
    pick,
    spread,
    place_own,
    place,
    table_grad,
    renew_grad,
    state_grad,
    cur,
    cur_pair,
    back_out,
    back_in,
    back_pair,
    acc,
    block_out,
    block_in,
    load_sem,
    feat_send,
    feat_recv,
    pack_send,
    pack_recv,
    feat_out,
    feat_in,
    pack_out,
    pack_in,
    req_send,
    req_recv,
    tab_send,
    tab_recv,
    list_send,
    list_recv,
    cur_send,
    cur_recv,
    back_send,
    back_recv,
    pass_send,
    pass_recv,
    block_send,
    block_recv,
):
    shards = n_node * n_event
    node, event = lax.axis_index("node"), lax.axis_index("event")
    slots = feat_ref.shape[1]
    width = mem.shape[1]
    group_rows = mem.shape[0]
    asked = req_ref.shape[2]
    table_rows = n_node * asked
    events = shards * slots
    turns = events // chunk
    chips = n_event // 2
    chip, core = event // 2, event % 2
    sibling = event + 1 - 2 * core
    block = group_rows // n_event
    half = width // 2

    barrier = pltpu.get_barrier_semaphore()

    def to_node(k):
        return lax.rem(node + k, n_node)

    def to_event(k):
        return lax.rem(event + k, n_event)

    for k in range(1, n_node):
        pl.semaphore_signal(barrier, inc=1, device_id=(to_node(k), event), device_id_type=MESH)

    @pl.loop(1, n_event)
    def _(k):
        pl.semaphore_signal(barrier, inc=1, device_id=(node, to_event(k)), device_id_type=MESH)

    small = [
        pltpu.make_async_copy(ids_hbm[k], ids.at[k], load_sem.at[k]) for k in range(4)
    ] + [pltpu.make_async_copy(count_hbm, count, load_sem.at[4])]
    loads = [
        pltpu.make_async_copy(source, target, load_sem.at[5 + k])
        for k, (source, target) in enumerate(
            (
                (mem_hbm, mem),
                (win_hbm, win),
                (wst_hbm, wst),
                (wpair_hbm, wpair),
                (bias_hbm, bias),
                (freq_hbm, freq),
            )
        )
    ]
    own_list = pltpu.make_async_copy(req_ref.at[node], wanted.at[node], req_recv.at[node])
    own_feat = pltpu.make_async_copy(
        feat_ref.at[pl.ds(node * n_event, n_event)], feats_relay.at[node], feat_recv.at[node]
    )
    for load in small + loads + [own_list, own_feat]:
        load.start()
    pl.semaphore_wait(barrier, n_node + n_event - 2)

    def arrived(buffer, sem, slot):
        pltpu.make_async_copy(buffer.at[slot], buffer.at[slot], sem.at[slot]).wait()

    def request_copy(k):
        peer = to_node(k)
        return pltpu.make_async_remote_copy(
            src_ref=req_ref.at[peer],
            dst_ref=wanted.at[node],
            send_sem=req_send.at[peer],
            recv_sem=req_recv.at[node],
            device_id=(peer, event),
            device_id_type=MESH,
        )

    for k in range(n_node - 1, 0, -1):
        request_copy(k).start()

    def to_group(k, source, target, send_sem, recv_sem):
        peer = to_node(k)
        return pltpu.make_async_remote_copy(
            src_ref=source.at[pl.ds(peer * n_event, n_event)],
            dst_ref=target.at[node],
            send_sem=send_sem.at[peer],
            recv_sem=recv_sem.at[node],
            device_id=(peer, event),
            device_id_type=MESH,
        )

    def group_copies(k):
        return (
            to_group(k, pack, packs_relay, pack_send, pack_recv),
            to_group(k, feat_ref, feats_relay, feat_send, feat_recv),
        )

    for k in range(n_node - 1, 0, -1):
        group_copies(k)[1].start()
    stage[...] = jnp.zeros_like(stage)
    for load in small:
        load.wait()
    for k in range(4):
        stage[k * slots : (k + 1) * slots, :shards] = ids[k]
    slot = lax.broadcasted_iota(jnp.int32, (slots, shards), 0)
    stage[4 * slots : 5 * slots, :shards] = jnp.where(slot < count[...], 1, 0)
    pack[...] = stage[...].T[:shards].reshape(shards, 1, LANES)
    packs_relay[node] = pack[pl.ds(node * n_event, n_event)]
    for k in range(n_node - 1, 0, -1):
        group_copies(k)[0].start()

    def table_copy(k):
        peer = to_node(k)
        return pltpu.make_async_remote_copy(
            src_ref=fetched.at[peer],
            dst_ref=table.at[node],
            send_sem=tab_send.at[peer],
            recv_sem=tab_recv.at[node],
            device_id=(peer, event),
            device_id_type=MESH,
        )

    def fetch(k):
        asker = to_node(k)
        arrived(wanted, req_recv, asker)
        column = jnp.broadcast_to(wanted[asker], (LANES, asked)).T
        return mm(pick_matrix(column, group_rows), mem[...]).astype(BF)

    loads[0].wait()
    for k in range(n_node - 1, 0, -1):
        fetched[to_node(k)] = fetch(k)
        table_copy(k).start()
    table[node] = fetch(0)

    def to_sibling(source, target, send_sem, recv_sem):
        return pltpu.make_async_remote_copy(
            src_ref=source,
            dst_ref=target,
            send_sem=send_sem,
            recv_sem=recv_sem,
            device_id=(node, sibling),
            device_id_type=MESH,
        )

    wanted_copy = to_sibling(wanted, wanted_pair, list_send.at[0], list_recv.at[0])
    wanted_copy.start()

    def to_owner(k, source, target, send_sem, recv_sem):
        peer = to_event(k)
        return pltpu.make_async_remote_copy(
            src_ref=source.at[:, peer],
            dst_ref=target.at[:, event],
            send_sem=send_sem.at[peer],
            recv_sem=recv_sem.at[event],
            device_id=(node, peer),
            device_id_type=MESH,
        )

    def owner_copies(k):
        return (
            to_owner(k, packs_relay, packs, pack_out, pack_in),
            to_owner(k, feats_relay, feats, feat_out, feat_in),
        )

    for k in range(n_node):
        if k > 0:
            arrived(packs_relay, pack_recv, to_node(k))
        arrived(feats_relay, feat_recv, to_node(k))

    @pl.loop(1, n_event)
    def _(k):
        for copy in owner_copies(k):
            copy.start()

    kept = [
        pltpu.make_async_copy(packs_relay.at[:, event], packs.at[:, event], pack_in.at[event]),
        pltpu.make_async_copy(feats_relay.at[:, event], feats.at[:, event], feat_in.at[event]),
    ]
    for copy in kept:
        copy.start()

    for load in loads[1:]:
        load.wait()

    @pl.loop(0, n_event)
    def _(e):
        for buffer, sem in ((packs, pack_in), (feats, feat_in)):
            pltpu.make_async_copy(buffer.at[:, e], buffer.at[:, e], sem.at[e]).wait()

    codes = packs[...].reshape(shards, LANES)
    code_parts = jnp.concatenate([codes >> 8, codes & 255], axis=1).astype(F32).astype(BF)
    kinds = 5
    from_lane = lax.broadcasted_iota(jnp.int32, (2 * LANES, kinds * LANES), 0)
    to_kind = lax.broadcasted_iota(jnp.int32, (2 * LANES, kinds * LANES), 1) // LANES
    weight = jnp.where(from_lane < LANES, 256.0, 1.0)
    gather_kind = jnp.where((from_lane % LANES) // slots == to_kind, weight, 0.0).astype(BF)
    bias_row = jnp.concatenate([bias[k : k + 1, :] for k in range(bias.shape[0])], axis=1)

    @pl.loop(0, turns)
    def _(t):
        first = t * (chunk // slots)
        home = lax.broadcasted_iota(jnp.int32, (chunk, shards), 0) // slots + first
        from_home = one_hot(home == lax.broadcasted_iota(jnp.int32, (chunk, shards), 1))
        mine = mm(from_home, code_parts)
        lane = lax.broadcasted_iota(jnp.int32, (chunk, 2 * LANES), 1)
        row = lax.broadcasted_iota(jnp.int32, (chunk, 2 * LANES), 0)
        mine = jnp.where(lane % slots == row % slots, mine, 0.0).astype(BF)
        columns = mm(mine, gather_kind)
        times = columns[:, 3 * LANES : 4 * LANES]
        live[t] = columns[:, 4 * LANES :]
        for kind in range(2):
            line = columns[:, (kind + 1) * LANES : (kind + 2) * LANES].T
            ids_row[t, kind] = line[:8].astype(jnp.int32)
        source_row[t] = columns[:, :LANES].T[:8].astype(jnp.int32)
        source = columns[:, :LANES].astype(jnp.int32)
        current = mm(pick_matrix(source, group_rows), mem[...]).astype(BF)
        from_state = mm(current, wst[...])
        timing = cosine(times * freq[...]).astype(BF)
        groups = chunk // (slots * n_event)
        feature = feats[pl.ds(t * groups, groups)].reshape(chunk, feat_ref.shape[2])
        from_rest = mm(jnp.concatenate([feature, timing], axis=1), win[width:, :])
        prev[t] = current
        recur[t] = from_state[:, 2 * width :]
        gates = from_rest[:, : 2 * width] + from_state[:, : 2 * width]
        pre[t] = jnp.concatenate([gates, from_rest[:, 2 * width :]], axis=1) + bias_row
        for kind in range(2):
            column = columns[:, (kind + 1) * LANES : (kind + 2) * LANES].astype(jnp.int32)
            pick[t, kind * chunk : (kind + 1) * chunk] = pick_matrix(column, table_rows)
            spread[t, :, kind * chunk : (kind + 1) * chunk] = spread_matrix(
                ids_row[t, kind][:1], table_rows, 0
            )

    source_copy = to_sibling(source_row, source_pair, list_send.at[1], list_recv.at[1])
    source_copy.start()
    for k in range(1, n_node):
        arrived(table, tab_recv, to_node(k))
    table_grad[...] = jnp.zeros_like(table_grad)
    factor = 1.0 / math.sqrt(width)

    @pl.loop(0, turns)
    def _(t):
        rows = mm(pick[t], table[...].reshape(table_rows, width)).astype(BF)
        partner = rows[:chunk]
        valid = live[t][:, :1]
        all_pre = pre[t] + mm(partner, win[:width, :])
        recurrent = recur[t]
        previous = prev[t].astype(F32)
        reset = sigmoid(all_pre[:, :width])
        update = sigmoid(all_pre[:, width : 2 * width])
        candidate = jnp.tanh(all_pre[:, 2 * width :] + reset * recurrent)
        renewed = (1.0 - update) * candidate + update * previous
        keys = mm(rows, wpair[...])
        key_pos, key_neg = keys[:chunk], keys[chunk:]
        score_pos = jnp.sum(renewed * key_pos, axis=1, keepdims=True) * factor
        score_neg = jnp.sum(renewed * key_neg, axis=1, keepdims=True) * factor
        weight_pos = -valid * jax.nn.sigmoid(-score_pos)
        weight_neg = valid * jax.nn.sigmoid(score_neg)
        grad_renewed = (weight_pos * key_pos + weight_neg * key_neg) * factor
        grad_keypos = (weight_pos * renewed * factor).astype(BF)
        grad_keyneg = (weight_neg * renewed * factor).astype(BF)
        grad_cand = grad_renewed * (1.0 - update) * (1.0 - candidate * candidate)
        grad_reset = (grad_cand * recurrent * reset * (1.0 - reset)).astype(BF)
        grad_update = (
            grad_renewed * (previous - candidate) * update * (1.0 - update)
        ).astype(BF)
        input_back = jnp.concatenate([grad_reset, grad_update, grad_cand.astype(BF)], axis=1)
        renew_grad[t] = grad_renewed * update
        state_grad[t] = jnp.concatenate(
            [grad_reset, grad_update, (grad_cand * reset).astype(BF)], axis=1
        )
        grad_keys = mm_nt(jnp.concatenate([grad_keypos, grad_keyneg], axis=0), wpair[...])
        grad_partner = mm_nt(input_back, win[:width, :]) + grad_keys[:chunk]
        high, low = split(jnp.concatenate([grad_partner, grad_keys[chunk:]], axis=0))
        table_grad[...] += mm(spread[t], high) + mm(spread[t], low)

    high, low = split(table_grad[...])
    for h in range(2):
        back_out[h] = high[:, h * half : (h + 1) * half].reshape(n_node, asked, half)

    def back_copy(h, k):
        peer = to_node(k)
        return pltpu.make_async_remote_copy(
            src_ref=back_out.at[h, peer],
            dst_ref=back_in.at[h, node],
            send_sem=back_send.at[h, peer],
            recv_sem=back_recv.at[h, node],
            device_id=(peer, event),
            device_id_type=MESH,
        )

    def pass_copy(h, slot):
        return to_sibling(
            back_in.at[h, slot],
            back_pair.at[h, slot],
            pass_send.at[h, slot],
            pass_recv.at[h, slot],
        )

    for h in range(2):
        for k in range(n_node - 1, 0, -1):
            back_copy(h, k).start()
    table_grad[...] = low.astype(F32)
    own_low = table_grad[pl.ds(pl.multiple_of(node * asked, asked), asked), :].astype(BF)
    for h in range(2):
        back_in[h, node] = back_out[h, node]
        back_in[h, n_node] = own_low[:, h * half : (h + 1) * half]
        pass_copy(h, node).start()
        pass_copy(h, n_node).start()

    @pl.loop(0, turns)
    def _(t):
        high, low = split(renew_grad[t] + mm_nt(state_grad[t], wst[...]))
        cur[t, 0] = high
        cur[t, 1] = low

    cur_copy = to_sibling(cur, cur_pair, cur_send, cur_recv)
    cur_copy.start()
    arrived_pair = pltpu.make_async_copy(wanted_pair, wanted_pair, list_recv.at[0])
    arrived_pair.wait()
    listed_own = jnp.concatenate([wanted[node]] * 2 + [wanted_pair[node]] * 2, axis=1)
    listed = jnp.concatenate(
        [wanted[to_node(k)] for k in range(1, n_node)]
        + [wanted_pair[to_node(k)] for k in range(1, n_node)],
        axis=1,
    )

    @pl.loop(0, chips)
    def _(j):
        base = (2 * j + core) * block
        place_own[j] = spread_matrix(listed_own, block, base)
        place[j] = spread_matrix(listed, block, base)

    @pl.loop(0, chips)
    def _(j):
        total = jnp.zeros((block, width), F32)
        for t in range(turns):
            at = spread_matrix(source_row[t][:1], block, (2 * j + core) * block)
            total += mm(at, cur[t, 0]) + mm(at, cur[t, 1])
        acc[j] = total

    for h in range(2):
        arrived(back_pair.at[h], pass_recv.at[h], node)
        arrived(back_pair.at[h], pass_recv.at[h], n_node)
    own_rows = jnp.concatenate(
        [
            jnp.concatenate([held[0, at], held[1, at]], axis=1)
            for held in (back_in, back_pair)
            for at in (node, n_node)
        ],
        axis=0,
    )
    pltpu.make_async_copy(source_pair, source_pair, list_recv.at[1]).wait()
    pltpu.make_async_copy(cur_pair, cur_pair, cur_recv).wait()

    @pl.loop(0, chips)
    def _(j):
        total = acc[j] + mm(place_own[j], own_rows)
        for t in range(turns):
            at = spread_matrix(source_pair[t][:1], block, (2 * j + core) * block)
            total += mm(at, cur_pair[t, 0]) + mm(at, cur_pair[t, 1])
        acc[j] = total

    def block_copy(h, j):
        return pltpu.make_async_remote_copy(
            src_ref=block_out.at[h, j],
            dst_ref=block_in.at[h, chip],
            send_sem=block_send.at[h, j],
            recv_sem=block_recv.at[h, chip],
            device_id=(node, 2 * j + core),
            device_id_type=MESH,
        )

    own = []
    for h in range(2):
        for k in range(1, n_node):
            slot = to_node(k)
            arrived(back_in.at[h], back_recv.at[h], slot)
            pass_copy(h, slot).start()
        for k in range(1, n_node):
            arrived(back_pair.at[h], pass_recv.at[h], to_node(k))
        returned = jnp.concatenate(
            [held[h, to_node(k)] for held in (back_in, back_pair) for k in range(1, n_node)],
            axis=0,
        )

        def whole_block(j):
            return acc[j][:, h * half : (h + 1) * half] + mm(place[j], returned)

        @pl.loop(1, chips)
        def _(k):
            j = lax.rem(chip + k, chips)
            block_out[h, j] = whole_block(j).astype(BF)
            block_copy(h, j).start()

        own.append(whole_block(chip))

    for h in range(2):
        total = own[h]
        for k in range(1, chips):
            j = lax.rem(chip + k, chips)
            arrived(block_in.at[h], block_recv.at[h], j)
            total += block_in[h, j].astype(F32)
        out_ref[:, h * half : (h + 1) * half] = total

    for k in range(1, n_node):
        request_copy(k).wait_send()
        table_copy(k).wait_send()
    for h in range(2):
        for k in range(1, n_node):
            back_copy(h, k).wait_send()
        for slot in range(n_node + 1):
            pass_copy(h, slot).wait_send()
        for k in range(1, chips):
            block_copy(h, lax.rem(chip + k, chips)).wait_send()
    wanted_copy.wait_send()
    source_copy.wait_send()
    cur_copy.wait_send()
    for k in range(1, n_node):
        for copy in group_copies(k):
            copy.wait_send()

    @pl.loop(1, n_event)
    def _(k):
        for copy in owner_copies(k):
            copy.wait_send()


def local(
    memory,
    event_feat,
    event_source,
    event_partner,
    event_negative,
    event_time,
    event_count,
    requests,
    w_input,
    w_state,
    w_pair,
    gate_bias,
    time_freq,
):
    n_node = lax.axis_size("node")
    n_event = lax.axis_size("event")
    shards = n_node * n_event
    slots, feat_width = event_feat.shape[2:]
    group_rows, width = memory.shape
    asked = requests.shape[2]
    table_rows = n_node * asked
    events = shards * slots
    chunk = math.gcd(events, 512)
    turns = events // chunk
    chips = n_event // 2
    block = group_rows // n_event
    half = width // 2
    listed = (n_node - 1) * asked
    bias_rows = gate_bias.shape[0] // LANES

    vmem = pl.BlockSpec(memory_space=pltpu.VMEM)
    hbm = pl.BlockSpec(memory_space=pl.ANY)
    dma = pltpu.SemaphoreType.DMA
    ids = [value[0].T for value in (event_source, event_partner, event_negative, event_time)]
    return pl.pallas_call(
        functools.partial(kernel, n_node, n_event, chunk),
        out_shape=OUT((block, width), F32),
        in_specs=[[hbm] * 4] + [hbm] * 9,
        out_specs=vmem,
        scratch_shapes=[
            pltpu.VMEM(memory.shape, BF),
            pltpu.VMEM(w_input.shape, BF),
            pltpu.VMEM(w_state.shape, BF),
            pltpu.VMEM(w_pair.shape, BF),
            pltpu.VMEM((bias_rows, LANES), F32),
            pltpu.VMEM((1, LANES), F32),
            pltpu.VMEM((4, slots, shards), jnp.int32),
            pltpu.VMEM((1, shards), jnp.int32),
            pltpu.VMEM((LANES, max(shards, LANES)), jnp.int32),
            pltpu.VMEM((shards, 1, LANES), jnp.int32),
            pltpu.VMEM((n_node, n_event, slots, feat_width), BF),
            pltpu.VMEM((n_node, n_event, 1, LANES), jnp.int32),
            pltpu.VMEM((n_node, n_event, slots, feat_width), BF),
            pltpu.VMEM((n_node, n_event, 1, LANES), jnp.int32),
            pltpu.VMEM((n_node, 1, asked), jnp.int32),
            pltpu.VMEM((n_node, 1, asked), jnp.int32),
            pltpu.VMEM((n_node, asked, width), BF),
            pltpu.VMEM((n_node, asked, width), BF),
            pltpu.VMEM((turns, chunk, 3 * width), F32),
            pltpu.VMEM((turns, chunk, width), F32),
            pltpu.VMEM((turns, chunk, width), BF),
            pltpu.VMEM((turns, 2, 8, chunk), jnp.int32),
            pltpu.VMEM((turns, 8, chunk), jnp.int32),
            pltpu.VMEM((turns, 8, chunk), jnp.int32),
            pltpu.VMEM((turns, chunk, LANES), F32),
            pltpu.VMEM((turns, 2 * chunk, table_rows), BF),
            pltpu.VMEM((turns, table_rows, 2 * chunk), BF),
            pltpu.VMEM((chips, block, 4 * asked), BF),
            pltpu.VMEM((chips, block, 2 * listed), BF),
            pltpu.VMEM((table_rows, width), F32),
            pltpu.VMEM((turns, chunk, width), F32),
            pltpu.VMEM((turns, chunk, 3 * width), BF),
            pltpu.VMEM((turns, 2, chunk, width), BF),
            pltpu.VMEM((turns, 2, chunk, width), BF),
            pltpu.VMEM((2, n_node, asked, half), BF),
            pltpu.VMEM((2, n_node + 1, asked, half), BF),
            pltpu.VMEM((2, n_node + 1, asked, half), BF),
            pltpu.VMEM((chips, block, width), F32),
            pltpu.VMEM((2, chips, block, half), BF),
            pltpu.VMEM((2, chips, block, half), BF),
            dma((11,)),
            dma((n_node,)),
            dma((n_node,)),
            dma((n_node,)),
            dma((n_node,)),
            dma((n_event,)),
            dma((n_event,)),
            dma((n_event,)),
            dma((n_event,)),
            dma((n_node,)),
            dma((n_node,)),
            dma((n_node,)),
            dma((n_node,)),
            dma((2,)),
            dma((2,)),
            dma,
            dma,
            dma((2, n_node)),
            dma((2, n_node)),
            dma((2, n_node + 1)),
            dma((2, n_node + 1)),
            dma((2, chips)),
            dma((2, chips)),
        ],
        compiler_params=pltpu.CompilerParams(
            collective_id=0, has_side_effects=True, vmem_limit_bytes=60 * 1024 * 1024
        ),
        name="memory_step",
    )(
        ids,
        event_count,
        event_feat[0],
        requests[0][:, None, :],
        memory,
        w_input,
        w_state,
        w_pair,
        gate_bias.reshape(bias_rows, LANES),
        time_freq[None, :],
    )


def solution(mesh):
    by_device = ("node", "event")
    in_specs = (
        P("node", None),
        P(by_device, None, None, None),
        P(by_device, None, None),
        P(by_device, None, None),
        P(by_device, None, None),
        P(by_device, None, None),
        P(by_device, None),
        P(by_device, None, None),
        P(),
        P(),
        P(),
        P(),
        P(),
    )
    out_specs = P(by_device, None)
    return jax.shard_map(local, mesh=mesh, in_specs=in_specs, out_specs=out_specs, check_vma=False)
```

```python
import functools
import math

import jax
import jax.numpy as jnp
from jax import lax
from jax.experimental import pallas as pl
from jax.experimental.pallas import tpu as pltpu
from jax.sharding import PartitionSpec as P

MESH = pl.DeviceIdType.MESH
BF = jnp.bfloat16
F32 = jnp.float32
LANES = 128
OUT = pltpu.VMEM


def mm(a, b):
    return jnp.dot(a, b, preferred_element_type=F32)


def mm_nt(a, b):
    return lax.dot_general(a, b, (((1,), (1,)), ((), ())), preferred_element_type=F32)


def split(value):
    high = value.astype(BF)
    return high, (value - high.astype(F32)).astype(BF)


def one_hot(mask):
    return jnp.where(mask, 1.0, 0.0).astype(BF)


def pick_matrix(column, total):
    lane = lax.broadcasted_iota(jnp.int32, column.shape, 1)
    return jnp.concatenate(
        [one_hot(column == lane + start) for start in range(0, total, LANES)], axis=1
    )


def spread_matrix(row, total, base):
    ids = lax.broadcasted_iota(jnp.int32, (total, row.shape[1]), 0) + base
    return one_hot(ids == row)


def sigmoid(value):
    return 0.5 * jnp.tanh(0.5 * value) + 0.5


def cosine(value):
    turns = jnp.floor(value * (1.0 / math.pi) + 0.5)
    rest = (value - turns * 3.140625) - turns * (math.pi - 3.140625)
    square = rest * rest
    series = jnp.full_like(value, 1.0 / math.factorial(12))
    for power in range(10, -1, -2):
        sign = 1.0 if power % 4 == 0 else -1.0
        series = series * square + sign / math.factorial(power)
    odd = turns - 2.0 * jnp.floor(0.5 * turns)
    return series * (1.0 - 2.0 * odd)


def each_turn(turns):
    if turns == 1:
        return lambda body: body(0)
    return pl.loop(0, turns)


def kernel(
    n_node,
    n_event,
    chunk,
    ids_hbm,
    count_hbm,
    feat_ref,
    req_ref,
    mem_hbm,
    win_hbm,
    wst_hbm,
    wpair_hbm,
    bias_hbm,
    freq_hbm,
    out_ref,
    mem,
    win,
    wst,
    wpair,
    bias,
    freq,
    ids,
    count,
    stage,
    gather_kind,
    same_slot,
    pack,
    feats_relay,
    packs_relay,
    feats,
    packs,
    wanted,
    wanted_pair,
    fetched,
    table,
    pre,
    recur,
    prev,
    ids_row,
    source_row,
    source_pair,
    live,
    pick,
    spread,
    place_own,
    place,
    table_grad,
    renew_grad,
    state_grad,
    cur,
    cur_pair,
    back_out,
    back_in,
    back_pair,
    acc,
    block_out,
    block_in,
    load_sem,
    feat_send,
    feat_recv,
    pack_send,
    pack_recv,
    feat_out,
    feat_in,
    pack_out,
    pack_in,
    req_send,
    req_recv,
    tab_send,
    tab_recv,
    list_send,
    list_recv,
    cur_send,
    cur_recv,
    back_send,
    back_recv,
    pass_send,
    pass_recv,
    block_send,
    block_recv,
):
    shards = n_node * n_event
    node, event = lax.axis_index("node"), lax.axis_index("event")
    slots = feat_ref.shape[1]
    width = mem.shape[1]
    group_rows = mem.shape[0]
    asked = req_ref.shape[2]
    table_rows = n_node * asked
    events = shards * slots
    turns = events // chunk
    chips = n_event // 2
    chip, core = event // 2, event % 2
    sibling = event + 1 - 2 * core
    block = group_rows // n_event
    half = width // 2

    barrier = pltpu.get_barrier_semaphore()

    def to_node(k):
        return lax.rem(node + k, n_node)

    def to_event(k):
        return lax.rem(event + k, n_event)

    for k in range(1, n_node):
        pl.semaphore_signal(barrier, inc=1, device_id=(to_node(k), event), device_id_type=MESH)

    @pl.loop(1, n_event)
    def _(k):
        pl.semaphore_signal(barrier, inc=1, device_id=(node, to_event(k)), device_id_type=MESH)

    small = [
        pltpu.make_async_copy(ids_hbm[k], ids.at[k], load_sem.at[k]) for k in range(4)
    ] + [pltpu.make_async_copy(count_hbm, count, load_sem.at[4])]
    loads = [
        pltpu.make_async_copy(source, target, load_sem.at[5 + k])
        for k, (source, target) in enumerate(
            (
                (mem_hbm, mem),
                (win_hbm, win),
                (wst_hbm, wst),
                (wpair_hbm, wpair),
                (bias_hbm, bias),
                (freq_hbm, freq),
            )
        )
    ]
    own_list = pltpu.make_async_copy(req_ref.at[node], wanted.at[node], req_recv.at[node])
    own_feat = pltpu.make_async_copy(
        feat_ref.at[pl.ds(node * n_event, n_event)], feats_relay.at[node], feat_recv.at[node]
    )
    for load in small + loads + [own_list, own_feat]:
        load.start()
    slot_bits = slots.bit_length() - 1
    kinds = 5
    from_lane = lax.broadcasted_iota(jnp.int32, (2 * LANES, kinds * LANES), 0)
    to_kind = lax.broadcasted_iota(jnp.int32, (2 * LANES, kinds * LANES), 1) >> 7
    weight = jnp.where(from_lane < LANES, 256.0, 1.0)
    same_kind = (from_lane & (LANES - 1)) >> slot_bits == to_kind
    gather_kind[...] = jnp.where(same_kind, weight, 0.0).astype(BF)
    lane = lax.broadcasted_iota(jnp.int32, (chunk, 2 * LANES), 1)
    row = lax.broadcasted_iota(jnp.int32, (chunk, 2 * LANES), 0)
    same_slot[...] = jnp.where(((lane ^ row) & (slots - 1)) == 0, 1.0, 0.0)
    pl.semaphore_wait(barrier, n_node + n_event - 2)

    def arrived(buffer, sem, slot):
        pltpu.make_async_copy(buffer.at[slot], buffer.at[slot], sem.at[slot]).wait()

    def request_copy(k):
        peer = to_node(k)
        return pltpu.make_async_remote_copy(
            src_ref=req_ref.at[peer],
            dst_ref=wanted.at[node],
            send_sem=req_send.at[peer],
            recv_sem=req_recv.at[node],
            device_id=(peer, event),
            device_id_type=MESH,
        )

    for k in range(n_node - 1, 0, -1):
        request_copy(k).start()

    def to_group(k, source, target, send_sem, recv_sem):
        peer = to_node(k)
        return pltpu.make_async_remote_copy(
            src_ref=source.at[pl.ds(peer * n_event, n_event)],
            dst_ref=target.at[node],
            send_sem=send_sem.at[peer],
            recv_sem=recv_sem.at[node],
            device_id=(peer, event),
            device_id_type=MESH,
        )

    def group_copies(k):
        return (
            to_group(k, pack, packs_relay, pack_send, pack_recv),
            to_group(k, feat_ref, feats_relay, feat_send, feat_recv),
        )

    for k in range(n_node - 1, 0, -1):
        group_copies(k)[1].start()
    stage[...] = jnp.zeros_like(stage)
    for load in small:
        load.wait()
    for k in range(4):
        stage[k * slots : (k + 1) * slots, :shards] = ids[k]
    slot = lax.broadcasted_iota(jnp.int32, (slots, shards), 0)
    stage[4 * slots : 5 * slots, :shards] = jnp.where(slot < count[...], 1, 0)
    pack[...] = stage[...].T[:shards].reshape(shards, 1, LANES)
    packs_relay[node] = pack[pl.ds(node * n_event, n_event)]
    for k in range(n_node - 1, 0, -1):
        group_copies(k)[0].start()

    def table_copy(k):
        peer = to_node(k)
        return pltpu.make_async_remote_copy(
            src_ref=fetched.at[peer],
            dst_ref=table.at[node],
            send_sem=tab_send.at[peer],
            recv_sem=tab_recv.at[node],
            device_id=(peer, event),
            device_id_type=MESH,
        )

    for k in range(n_node):
        arrived(wanted, req_recv, to_node(k))
    columns = [jnp.broadcast_to(wanted[g], (LANES, asked)).T for g in range(n_node)]
    loads[0].wait()
    picked = mm(pick_matrix(jnp.concatenate(columns, axis=0), group_rows), mem[...]).astype(BF)
    fetched[...] = picked.reshape(n_node, asked, width)
    for k in range(n_node - 1, 0, -1):
        table_copy(k).start()
    table[node] = fetched[node]

    def to_sibling(source, target, send_sem, recv_sem):
        return pltpu.make_async_remote_copy(
            src_ref=source,
            dst_ref=target,
            send_sem=send_sem,
            recv_sem=recv_sem,
            device_id=(node, sibling),
            device_id_type=MESH,
        )

    wanted_copy = to_sibling(wanted, wanted_pair, list_send.at[0], list_recv.at[0])
    wanted_copy.start()

    def to_owner(k, source, target, send_sem, recv_sem):
        peer = to_event(k)
        return pltpu.make_async_remote_copy(
            src_ref=source.at[:, peer],
            dst_ref=target.at[:, event],
            send_sem=send_sem.at[peer],
            recv_sem=recv_sem.at[event],
            device_id=(node, peer),
            device_id_type=MESH,
        )

    def owner_copies(k):
        return (
            to_owner(k, packs_relay, packs, pack_out, pack_in),
            to_owner(k, feats_relay, feats, feat_out, feat_in),
        )

    for k in range(n_node):
        if k > 0:
            arrived(packs_relay, pack_recv, to_node(k))
        arrived(feats_relay, feat_recv, to_node(k))

    @pl.loop(1, n_event)
    def _(k):
        for copy in owner_copies(k):
            copy.start()

    kept = [
        pltpu.make_async_copy(packs_relay.at[:, event], packs.at[:, event], pack_in.at[event]),
        pltpu.make_async_copy(feats_relay.at[:, event], feats.at[:, event], feat_in.at[event]),
    ]
    for copy in kept:
        copy.start()

    for load in loads[1:]:
        load.wait()

    @pl.loop(0, n_event)
    def _(e):
        for buffer, sem in ((packs, pack_in), (feats, feat_in)):
            pltpu.make_async_copy(buffer.at[:, e], buffer.at[:, e], sem.at[e]).wait()

    codes = packs[...].reshape(shards, LANES)
    code_parts = jnp.concatenate([codes >> 8, codes & 255], axis=1).astype(F32).astype(BF)
    bias_row = jnp.concatenate([bias[k : k + 1, :] for k in range(bias.shape[0])], axis=1)

    @each_turn(turns)
    def _(t):
        first = t * (chunk // slots)
        home = (lax.broadcasted_iota(jnp.int32, (chunk, shards), 0) >> slot_bits) + first
        from_home = one_hot(home == lax.broadcasted_iota(jnp.int32, (chunk, shards), 1))
        mine = (mm(from_home, code_parts) * same_slot[...]).astype(BF)
        columns = mm(mine, gather_kind[...])
        times = columns[:, 3 * LANES : 4 * LANES]
        live[t] = columns[:, 4 * LANES :]
        for kind in range(2):
            line = columns[:, (kind + 1) * LANES : (kind + 2) * LANES].T
            ids_row[t, kind] = line[:8].astype(jnp.int32)
        source_row[t] = columns[:, :LANES].T[:8].astype(jnp.int32)
        source = columns[:, :LANES].astype(jnp.int32)
        current = mm(pick_matrix(source, group_rows), mem[...]).astype(BF)
        from_state = mm(current, wst[...])
        timing = cosine(times * freq[...]).astype(BF)
        groups = chunk // (slots * n_event)
        feature = feats[pl.ds(t * groups, groups)].reshape(chunk, feat_ref.shape[2])
        from_rest = mm(jnp.concatenate([feature, timing], axis=1), win[width:, :])
        prev[t] = current
        recur[t] = from_state[:, 2 * width :]
        gates = from_rest[:, : 2 * width] + from_state[:, : 2 * width]
        pre[t] = jnp.concatenate([gates, from_rest[:, 2 * width :]], axis=1) + bias_row
        for kind in range(2):
            column = columns[:, (kind + 1) * LANES : (kind + 2) * LANES].astype(jnp.int32)
            pick[t, kind * chunk : (kind + 1) * chunk] = pick_matrix(column, table_rows)
            spread[t, :, kind * chunk : (kind + 1) * chunk] = spread_matrix(
                ids_row[t, kind][:1], table_rows, 0
            )

    source_copy = to_sibling(source_row, source_pair, list_send.at[1], list_recv.at[1])
    source_copy.start()
    for k in range(1, n_node):
        arrived(table, tab_recv, to_node(k))
    table_grad[...] = jnp.zeros_like(table_grad)
    factor = 1.0 / math.sqrt(width)

    @each_turn(turns)
    def _(t):
        rows = mm(pick[t], table[...].reshape(table_rows, width)).astype(BF)
        partner = rows[:chunk]
        valid = live[t][:, :1]
        all_pre = pre[t] + mm(partner, win[:width, :])
        recurrent = recur[t]
        previous = prev[t].astype(F32)
        reset = sigmoid(all_pre[:, :width])
        update = sigmoid(all_pre[:, width : 2 * width])
        candidate = jnp.tanh(all_pre[:, 2 * width :] + reset * recurrent)
        renewed = (1.0 - update) * candidate + update * previous
        keys = mm(rows, wpair[...])
        key_pos, key_neg = keys[:chunk], keys[chunk:]
        score_pos = jnp.sum(renewed * key_pos, axis=1, keepdims=True) * factor
        score_neg = jnp.sum(renewed * key_neg, axis=1, keepdims=True) * factor
        weight_pos = -valid * jax.nn.sigmoid(-score_pos)
        weight_neg = valid * jax.nn.sigmoid(score_neg)
        grad_renewed = (weight_pos * key_pos + weight_neg * key_neg) * factor
        grad_keypos = (weight_pos * renewed * factor).astype(BF)
        grad_keyneg = (weight_neg * renewed * factor).astype(BF)
        grad_cand = grad_renewed * (1.0 - update) * (1.0 - candidate * candidate)
        grad_reset = (grad_cand * recurrent * reset * (1.0 - reset)).astype(BF)
        grad_update = (
            grad_renewed * (previous - candidate) * update * (1.0 - update)
        ).astype(BF)
        input_back = jnp.concatenate([grad_reset, grad_update, grad_cand.astype(BF)], axis=1)
        renew_grad[t] = grad_renewed * update
        state_grad[t] = jnp.concatenate(
            [grad_reset, grad_update, (grad_cand * reset).astype(BF)], axis=1
        )
        grad_keys = mm_nt(jnp.concatenate([grad_keypos, grad_keyneg], axis=0), wpair[...])
        grad_partner = mm_nt(input_back, win[:width, :]) + grad_keys[:chunk]
        high, low = split(jnp.concatenate([grad_partner, grad_keys[chunk:]], axis=0))
        table_grad[...] += mm(spread[t], high) + mm(spread[t], low)

    high, low = split(table_grad[...])
    for h in range(2):
        back_out[h] = high[:, h * half : (h + 1) * half].reshape(n_node, asked, half)

    def back_copy(h, k):
        peer = to_node(k)
        return pltpu.make_async_remote_copy(
            src_ref=back_out.at[h, peer],
            dst_ref=back_in.at[h, node],
            send_sem=back_send.at[h, peer],
            recv_sem=back_recv.at[h, node],
            device_id=(peer, event),
            device_id_type=MESH,
        )

    def pass_copy(h, slot):
        return to_sibling(
            back_in.at[h, slot],
            back_pair.at[h, slot],
            pass_send.at[h, slot],
            pass_recv.at[h, slot],
        )

    for h in range(2):
        for k in range(n_node - 1, 0, -1):
            back_copy(h, k).start()
    table_grad[...] = low.astype(F32)
    own_low = table_grad[pl.ds(pl.multiple_of(node * asked, asked), asked), :].astype(BF)
    for h in range(2):
        back_in[h, node] = back_out[h, node]
        back_in[h, n_node] = own_low[:, h * half : (h + 1) * half]
        pass_copy(h, node).start()
        pass_copy(h, n_node).start()

    @each_turn(turns)
    def _(t):
        high, low = split(renew_grad[t] + mm_nt(state_grad[t], wst[...]))
        cur[t, 0] = high
        cur[t, 1] = low

    cur_copy = to_sibling(cur, cur_pair, cur_send, cur_recv)
    cur_copy.start()
    arrived_pair = pltpu.make_async_copy(wanted_pair, wanted_pair, list_recv.at[0])
    arrived_pair.wait()
    listed_own = jnp.concatenate([wanted[node]] * 2 + [wanted_pair[node]] * 2, axis=1)
    listed = jnp.concatenate(
        [wanted[to_node(k)] for k in range(1, n_node)]
        + [wanted_pair[to_node(k)] for k in range(1, n_node)],
        axis=1,
    )

    @pl.loop(0, chips)
    def _(j):
        base = (2 * j + core) * block
        place_own[j] = spread_matrix(listed_own, block, base)
        place[j] = spread_matrix(listed, block, base)

    @pl.loop(0, chips)
    def _(j):
        total = jnp.zeros((block, width), F32)
        for t in range(turns):
            at = spread_matrix(source_row[t][:1], block, (2 * j + core) * block)
            total += mm(at, cur[t, 0]) + mm(at, cur[t, 1])
        acc[j] = total

    for h in range(2):
        arrived(back_pair.at[h], pass_recv.at[h], node)
        arrived(back_pair.at[h], pass_recv.at[h], n_node)
    own_rows = jnp.concatenate(
        [
            jnp.concatenate([held[0, at], held[1, at]], axis=1)
            for held in (back_in, back_pair)
            for at in (node, n_node)
        ],
        axis=0,
    )
    pltpu.make_async_copy(source_pair, source_pair, list_recv.at[1]).wait()
    pltpu.make_async_copy(cur_pair, cur_pair, cur_recv).wait()

    @pl.loop(0, chips)
    def _(j):
        total = acc[j] + mm(place_own[j], own_rows)
        for t in range(turns):
            at = spread_matrix(source_pair[t][:1], block, (2 * j + core) * block)
            total += mm(at, cur_pair[t, 0]) + mm(at, cur_pair[t, 1])
        acc[j] = total

    def block_copy(h, j):
        return pltpu.make_async_remote_copy(
            src_ref=block_out.at[h, j],
            dst_ref=block_in.at[h, chip],
            send_sem=block_send.at[h, j],
            recv_sem=block_recv.at[h, chip],
            device_id=(node, 2 * j + core),
            device_id_type=MESH,
        )

    own = []
    for h in range(2):
        for k in range(1, n_node):
            slot = to_node(k)
            arrived(back_in.at[h], back_recv.at[h], slot)
            pass_copy(h, slot).start()
        for k in range(1, n_node):
            arrived(back_pair.at[h], pass_recv.at[h], to_node(k))
        returned = jnp.concatenate(
            [held[h, to_node(k)] for held in (back_in, back_pair) for k in range(1, n_node)],
            axis=0,
        )

        def whole_block(j):
            return acc[j][:, h * half : (h + 1) * half] + mm(place[j], returned)

        @pl.loop(1, chips)
        def _(k):
            j = lax.rem(chip + k, chips)
            block_out[h, j] = whole_block(j).astype(BF)
            block_copy(h, j).start()

        own.append(whole_block(chip))

    for h in range(2):
        total = own[h]
        for k in range(1, chips):
            j = lax.rem(chip + k, chips)
            arrived(block_in.at[h], block_recv.at[h], j)
            total += block_in[h, j].astype(F32)
        out_ref[:, h * half : (h + 1) * half] = total

    for k in range(1, n_node):
        request_copy(k).wait_send()
        table_copy(k).wait_send()
    for h in range(2):
        for k in range(1, n_node):
            back_copy(h, k).wait_send()
        for slot in range(n_node + 1):
            pass_copy(h, slot).wait_send()
        for k in range(1, chips):
            block_copy(h, lax.rem(chip + k, chips)).wait_send()
    wanted_copy.wait_send()
    source_copy.wait_send()
    cur_copy.wait_send()
    for k in range(1, n_node):
        for copy in group_copies(k):
            copy.wait_send()

    @pl.loop(1, n_event)
    def _(k):
        for copy in owner_copies(k):
            copy.wait_send()


def local(
    memory,
    event_feat,
    event_source,
    event_partner,
    event_negative,
    event_time,
    event_count,
    requests,
    w_input,
    w_state,
    w_pair,
    gate_bias,
    time_freq,
):
    n_node = lax.axis_size("node")
    n_event = lax.axis_size("event")
    shards = n_node * n_event
    slots, feat_width = event_feat.shape[2:]
    group_rows, width = memory.shape
    asked = requests.shape[2]
    table_rows = n_node * asked
    events = shards * slots
    chunk = math.gcd(events, 512)
    turns = events // chunk
    chips = n_event // 2
    block = group_rows // n_event
    half = width // 2
    listed = (n_node - 1) * asked
    bias_rows = gate_bias.shape[0] // LANES

    vmem = pl.BlockSpec(memory_space=pltpu.VMEM)
    hbm = pl.BlockSpec(memory_space=pl.ANY)
    dma = pltpu.SemaphoreType.DMA
    ids = [value[0].T for value in (event_source, event_partner, event_negative, event_time)]
    return pl.pallas_call(
        functools.partial(kernel, n_node, n_event, chunk),
        out_shape=OUT((block, width), F32),
        in_specs=[[hbm] * 4] + [hbm] * 9,
        out_specs=vmem,
        scratch_shapes=[
            pltpu.VMEM(memory.shape, BF),
            pltpu.VMEM(w_input.shape, BF),
            pltpu.VMEM(w_state.shape, BF),
            pltpu.VMEM(w_pair.shape, BF),
            pltpu.VMEM((bias_rows, LANES), F32),
            pltpu.VMEM((1, LANES), F32),
            pltpu.VMEM((4, slots, shards), jnp.int32),
            pltpu.VMEM((1, shards), jnp.int32),
            pltpu.VMEM((LANES, max(shards, LANES)), jnp.int32),
            pltpu.VMEM((2 * LANES, 5 * LANES), BF),
            pltpu.VMEM((chunk, 2 * LANES), F32),
            pltpu.VMEM((shards, 1, LANES), jnp.int32),
            pltpu.VMEM((n_node, n_event, slots, feat_width), BF),
            pltpu.VMEM((n_node, n_event, 1, LANES), jnp.int32),
            pltpu.VMEM((n_node, n_event, slots, feat_width), BF),
            pltpu.VMEM((n_node, n_event, 1, LANES), jnp.int32),
            pltpu.VMEM((n_node, 1, asked), jnp.int32),
            pltpu.VMEM((n_node, 1, asked), jnp.int32),
            pltpu.VMEM((n_node, asked, width), BF),
            pltpu.VMEM((n_node, asked, width), BF),
            pltpu.VMEM((turns, chunk, 3 * width), F32),
            pltpu.VMEM((turns, chunk, width), F32),
            pltpu.VMEM((turns, chunk, width), BF),
            pltpu.VMEM((turns, 2, 8, chunk), jnp.int32),
            pltpu.VMEM((turns, 8, chunk), jnp.int32),
            pltpu.VMEM((turns, 8, chunk), jnp.int32),
            pltpu.VMEM((turns, chunk, LANES), F32),
            pltpu.VMEM((turns, 2 * chunk, table_rows), BF),
            pltpu.VMEM((turns, table_rows, 2 * chunk), BF),
            pltpu.VMEM((chips, block, 4 * asked), BF),
            pltpu.VMEM((chips, block, 2 * listed), BF),
            pltpu.VMEM((table_rows, width), F32),
            pltpu.VMEM((turns, chunk, width), F32),
            pltpu.VMEM((turns, chunk, 3 * width), BF),
            pltpu.VMEM((turns, 2, chunk, width), BF),
            pltpu.VMEM((turns, 2, chunk, width), BF),
            pltpu.VMEM((2, n_node, asked, half), BF),
            pltpu.VMEM((2, n_node + 1, asked, half), BF),
            pltpu.VMEM((2, n_node + 1, asked, half), BF),
            pltpu.VMEM((chips, block, width), F32),
            pltpu.VMEM((2, chips, block, half), BF),
            pltpu.VMEM((2, chips, block, half), BF),
            dma((11,)),
            dma((n_node,)),
            dma((n_node,)),
            dma((n_node,)),
            dma((n_node,)),
            dma((n_event,)),
            dma((n_event,)),
            dma((n_event,)),
            dma((n_event,)),
            dma((n_node,)),
            dma((n_node,)),
            dma((n_node,)),
            dma((n_node,)),
            dma((2,)),
            dma((2,)),
            dma,
            dma,
            dma((2, n_node)),
            dma((2, n_node)),
            dma((2, n_node + 1)),
            dma((2, n_node + 1)),
            dma((2, chips)),
            dma((2, chips)),
        ],
        compiler_params=pltpu.CompilerParams(
            collective_id=0, has_side_effects=True, vmem_limit_bytes=60 * 1024 * 1024
        ),
        name="memory_step",
    )(
        ids,
        event_count,
        event_feat[0],
        requests[0][:, None, :],
        memory,
        w_input,
        w_state,
        w_pair,
        gate_bias.reshape(bias_rows, LANES),
        time_freq[None, :],
    )


def solution(mesh):
    by_device = ("node", "event")
    in_specs = (
        P("node", None),
        P(by_device, None, None, None),
        P(by_device, None, None),
        P(by_device, None, None),
        P(by_device, None, None),
        P(by_device, None, None),
        P(by_device, None),
        P(by_device, None, None),
        P(),
        P(),
        P(),
        P(),
        P(),
    )
    out_specs = P(by_device, None)
    return jax.shard_map(local, mesh=mesh, in_specs=in_specs, out_specs=out_specs, check_vma=False)
```

```python
import functools
import math

import jax
import jax.numpy as jnp
from jax import lax
from jax.experimental import pallas as pl
from jax.experimental.pallas import tpu as pltpu
from jax.sharding import PartitionSpec as P

MESH = pl.DeviceIdType.MESH
BF = jnp.bfloat16
F32 = jnp.float32
LANES = 128
OUT = pltpu.VMEM


def mm(a, b):
    return jnp.dot(a, b, preferred_element_type=F32)


def mm_nt(a, b):
    return lax.dot_general(a, b, (((1,), (1,)), ((), ())), preferred_element_type=F32)


def split(value):
    high = value.astype(BF)
    return high, (value - high.astype(F32)).astype(BF)


def one_hot(mask):
    return jnp.where(mask, 1.0, 0.0).astype(BF)


def pick_matrix(column, total):
    lane = lax.broadcasted_iota(jnp.int32, column.shape, 1)
    return jnp.concatenate(
        [one_hot(column == lane + start) for start in range(0, total, LANES)], axis=1
    )


def spread_matrix(row, total, base):
    ids = lax.broadcasted_iota(jnp.int32, (total, row.shape[1]), 0) + base
    return one_hot(ids == row)


def sigmoid(value):
    return 0.5 * jnp.tanh(0.5 * value) + 0.5


def cosine(value):
    turns = jnp.floor(value * (1.0 / math.pi) + 0.5)
    rest = (value - turns * 3.140625) - turns * (math.pi - 3.140625)
    square = rest * rest
    series = jnp.full_like(value, 1.0 / math.factorial(12))
    for power in range(10, -1, -2):
        sign = 1.0 if power % 4 == 0 else -1.0
        series = series * square + sign / math.factorial(power)
    odd = turns - 2.0 * jnp.floor(0.5 * turns)
    return series * (1.0 - 2.0 * odd)


def each_turn(turns):
    if turns == 1:
        return lambda body: body(0)
    return pl.loop(0, turns)


def kernel(
    n_node,
    n_event,
    chunk,
    ids_hbm,
    count_hbm,
    feat_ref,
    req_ref,
    mem_hbm,
    win_hbm,
    wst_hbm,
    wpair_hbm,
    bias_hbm,
    freq_hbm,
    out_ref,
    mem,
    win,
    wst,
    wpair,
    bias,
    freq,
    ids,
    count,
    stage,
    gather_kind,
    same_slot,
    pack,
    feats_relay,
    packs_relay,
    feats,
    packs,
    wanted,
    wanted_pair,
    fetched,
    table,
    pre,
    recur,
    prev,
    ids_row,
    source_row,
    source_pair,
    live,
    timing,
    pick,
    spread,
    place_own,
    place,
    table_grad,
    renew_grad,
    state_grad,
    cur,
    cur_pair,
    back_out,
    back_in,
    back_pair,
    acc,
    block_out,
    block_in,
    load_sem,
    feat_send,
    feat_recv,
    pack_send,
    pack_recv,
    feat_out,
    feat_in,
    pack_out,
    pack_in,
    req_send,
    req_recv,
    tab_send,
    tab_recv,
    list_send,
    list_recv,
    cur_send,
    cur_recv,
    back_send,
    back_recv,
    pass_send,
    pass_recv,
    block_send,
    block_recv,
):
    shards = n_node * n_event
    node, event = lax.axis_index("node"), lax.axis_index("event")
    slots = feat_ref.shape[1]
    width = mem.shape[1]
    group_rows = mem.shape[0]
    asked = req_ref.shape[2]
    table_rows = n_node * asked
    events = shards * slots
    turns = events // chunk
    chips = n_event // 2
    chip, core = event // 2, event % 2
    sibling = event + 1 - 2 * core
    block = group_rows // n_event
    half = width // 2

    barrier = pltpu.get_barrier_semaphore()

    def to_node(k):
        return lax.rem(node + k, n_node)

    def to_event(k):
        return lax.rem(event + k, n_event)

    for k in range(1, n_node):
        pl.semaphore_signal(barrier, inc=1, device_id=(to_node(k), event), device_id_type=MESH)

    @pl.loop(1, n_event)
    def _(k):
        pl.semaphore_signal(barrier, inc=1, device_id=(node, to_event(k)), device_id_type=MESH)

    small = [
        pltpu.make_async_copy(ids_hbm[k], ids.at[k], load_sem.at[k]) for k in range(4)
    ] + [pltpu.make_async_copy(count_hbm, count, load_sem.at[4])]
    loads = [
        pltpu.make_async_copy(source, target, load_sem.at[5 + k])
        for k, (source, target) in enumerate(
            (
                (mem_hbm, mem),
                (win_hbm, win),
                (wst_hbm, wst),
                (wpair_hbm, wpair),
                (bias_hbm, bias),
                (freq_hbm, freq),
            )
        )
    ]
    own_list = pltpu.make_async_copy(req_ref.at[node], wanted.at[node], req_recv.at[node])
    own_feat = pltpu.make_async_copy(
        feat_ref.at[pl.ds(node * n_event, n_event)], feats_relay.at[node], feat_recv.at[node]
    )
    for load in small + loads + [own_list, own_feat]:
        load.start()
    slot_bits = slots.bit_length() - 1
    kinds = 5
    from_lane = lax.broadcasted_iota(jnp.int32, (2 * LANES, kinds * LANES), 0)
    to_kind = lax.broadcasted_iota(jnp.int32, (2 * LANES, kinds * LANES), 1) >> 7
    weight = jnp.where(from_lane < LANES, 256.0, 1.0)
    same_kind = (from_lane & (LANES - 1)) >> slot_bits == to_kind
    gather_kind[...] = jnp.where(same_kind, weight, 0.0).astype(BF)
    lane = lax.broadcasted_iota(jnp.int32, (chunk, 2 * LANES), 1)
    row = lax.broadcasted_iota(jnp.int32, (chunk, 2 * LANES), 0)
    same_slot[...] = jnp.where(((lane ^ row) & (slots - 1)) == 0, 1.0, 0.0)
    pl.semaphore_wait(barrier, n_node + n_event - 2)

    def arrived(buffer, sem, slot):
        pltpu.make_async_copy(buffer.at[slot], buffer.at[slot], sem.at[slot]).wait()

    def request_copy(k):
        peer = to_node(k)
        return pltpu.make_async_remote_copy(
            src_ref=req_ref.at[peer],
            dst_ref=wanted.at[node],
            send_sem=req_send.at[peer],
            recv_sem=req_recv.at[node],
            device_id=(peer, event),
            device_id_type=MESH,
        )

    for k in range(n_node - 1, 0, -1):
        request_copy(k).start()

    def to_group(k, source, target, send_sem, recv_sem):
        peer = to_node(k)
        return pltpu.make_async_remote_copy(
            src_ref=source.at[pl.ds(peer * n_event, n_event)],
            dst_ref=target.at[node],
            send_sem=send_sem.at[peer],
            recv_sem=recv_sem.at[node],
            device_id=(peer, event),
            device_id_type=MESH,
        )

    def group_copies(k):
        return (
            to_group(k, pack, packs_relay, pack_send, pack_recv),
            to_group(k, feat_ref, feats_relay, feat_send, feat_recv),
        )

    stage[...] = jnp.zeros_like(stage)
    for load in small:
        load.wait()
    for k in range(4):
        stage[k * slots : (k + 1) * slots, :shards] = ids[k]
    slot = lax.broadcasted_iota(jnp.int32, (slots, shards), 0)
    stage[4 * slots : 5 * slots, :shards] = jnp.where(slot < count[...], 1, 0)
    pack[...] = stage[...].T[:shards].reshape(shards, 1, LANES)
    packs_relay[node] = pack[pl.ds(node * n_event, n_event)]
    for k in range(n_node - 1, 0, -1):
        group_copies(k)[0].start()
    for k in range(n_node - 1, 0, -1):
        group_copies(k)[1].start()

    def table_copy(k):
        peer = to_node(k)
        return pltpu.make_async_remote_copy(
            src_ref=fetched.at[peer],
            dst_ref=table.at[node],
            send_sem=tab_send.at[peer],
            recv_sem=tab_recv.at[node],
            device_id=(peer, event),
            device_id_type=MESH,
        )

    for k in range(n_node):
        arrived(wanted, req_recv, to_node(k))
    columns = [jnp.broadcast_to(wanted[g], (LANES, asked)).T for g in range(n_node)]
    loads[0].wait()
    picked = mm(pick_matrix(jnp.concatenate(columns, axis=0), group_rows), mem[...]).astype(BF)
    fetched[...] = picked.reshape(n_node, asked, width)
    for k in range(n_node - 1, 0, -1):
        table_copy(k).start()
    table[node] = fetched[node]

    def to_sibling(source, target, send_sem, recv_sem):
        return pltpu.make_async_remote_copy(
            src_ref=source,
            dst_ref=target,
            send_sem=send_sem,
            recv_sem=recv_sem,
            device_id=(node, sibling),
            device_id_type=MESH,
        )

    wanted_copy = to_sibling(wanted, wanted_pair, list_send.at[0], list_recv.at[0])
    wanted_copy.start()

    def to_owner(k, source, target, send_sem, recv_sem):
        peer = to_event(k)
        return pltpu.make_async_remote_copy(
            src_ref=source.at[:, peer],
            dst_ref=target.at[:, event],
            send_sem=send_sem.at[peer],
            recv_sem=recv_sem.at[event],
            device_id=(node, peer),
            device_id_type=MESH,
        )

    def owner_copies(k):
        return (
            to_owner(k, packs_relay, packs, pack_out, pack_in),
            to_owner(k, feats_relay, feats, feat_out, feat_in),
        )

    kept = [
        pltpu.make_async_copy(packs_relay.at[:, event], packs.at[:, event], pack_in.at[event]),
        pltpu.make_async_copy(feats_relay.at[:, event], feats.at[:, event], feat_in.at[event]),
    ]
    for k in range(1, n_node):
        arrived(packs_relay, pack_recv, to_node(k))

    @pl.loop(1, n_event)
    def _(k):
        owner_copies(k)[0].start()

    kept[0].start()
    for k in range(n_node):
        arrived(feats_relay, feat_recv, to_node(k))

    @pl.loop(1, n_event)
    def _(k):
        owner_copies(k)[1].start()

    kept[1].start()

    for load in loads[1:]:
        load.wait()

    @pl.loop(0, n_event)
    def _(e):
        pltpu.make_async_copy(packs.at[:, e], packs.at[:, e], pack_in.at[e]).wait()

    codes = packs[...].reshape(shards, LANES)
    code_parts = jnp.concatenate([codes >> 8, codes & 255], axis=1).astype(F32).astype(BF)
    bias_row = jnp.concatenate([bias[k : k + 1, :] for k in range(bias.shape[0])], axis=1)

    @each_turn(turns)
    def _(t):
        first = t * (chunk // slots)
        home = (lax.broadcasted_iota(jnp.int32, (chunk, shards), 0) >> slot_bits) + first
        from_home = one_hot(home == lax.broadcasted_iota(jnp.int32, (chunk, shards), 1))
        mine = (mm(from_home, code_parts) * same_slot[...]).astype(BF)
        columns = mm(mine, gather_kind[...])
        times = columns[:, 3 * LANES : 4 * LANES]
        live[t] = columns[:, 4 * LANES :]
        for kind in range(2):
            line = columns[:, (kind + 1) * LANES : (kind + 2) * LANES].T
            ids_row[t, kind] = line[:8].astype(jnp.int32)
        source_row[t] = columns[:, :LANES].T[:8].astype(jnp.int32)
        source = columns[:, :LANES].astype(jnp.int32)
        current = mm(pick_matrix(source, group_rows), mem[...]).astype(BF)
        from_state = mm(current, wst[...])
        timing[t] = cosine(times * freq[...]).astype(BF)
        prev[t] = current
        recur[t] = from_state[:, 2 * width :]
        gates = [from_state[:, : 2 * width], jnp.zeros((chunk, width), F32)]
        pre[t] = jnp.concatenate(gates, axis=1) + bias_row
        for kind in range(2):
            column = columns[:, (kind + 1) * LANES : (kind + 2) * LANES].astype(jnp.int32)
            pick[t, kind * chunk : (kind + 1) * chunk] = pick_matrix(column, table_rows)
            spread[t, :, kind * chunk : (kind + 1) * chunk] = spread_matrix(
                ids_row[t, kind][:1], table_rows, 0
            )

    @pl.loop(0, n_event)
    def _(e):
        pltpu.make_async_copy(feats.at[:, e], feats.at[:, e], feat_in.at[e]).wait()

    @each_turn(turns)
    def _(t):
        groups = chunk // (slots * n_event)
        feature = feats[pl.ds(t * groups, groups)].reshape(chunk, feat_ref.shape[2])
        pre[t] += mm(jnp.concatenate([feature, timing[t]], axis=1), win[width:, :])

    source_copy = to_sibling(source_row, source_pair, list_send.at[1], list_recv.at[1])
    source_copy.start()
    for k in range(1, n_node):
        arrived(table, tab_recv, to_node(k))
    table_grad[...] = jnp.zeros_like(table_grad)
    factor = 1.0 / math.sqrt(width)

    @each_turn(turns)
    def _(t):
        rows = mm(pick[t], table[...].reshape(table_rows, width)).astype(BF)
        partner = rows[:chunk]
        valid = live[t][:, :1]
        all_pre = pre[t] + mm(partner, win[:width, :])
        recurrent = recur[t]
        previous = prev[t].astype(F32)
        reset = sigmoid(all_pre[:, :width])
        update = sigmoid(all_pre[:, width : 2 * width])
        candidate = jnp.tanh(all_pre[:, 2 * width :] + reset * recurrent)
        renewed = (1.0 - update) * candidate + update * previous
        keys = mm(rows, wpair[...])
        key_pos, key_neg = keys[:chunk], keys[chunk:]
        score_pos = jnp.sum(renewed * key_pos, axis=1, keepdims=True) * factor
        score_neg = jnp.sum(renewed * key_neg, axis=1, keepdims=True) * factor
        weight_pos = -valid * jax.nn.sigmoid(-score_pos)
        weight_neg = valid * jax.nn.sigmoid(score_neg)
        grad_renewed = (weight_pos * key_pos + weight_neg * key_neg) * factor
        grad_keypos = (weight_pos * renewed * factor).astype(BF)
        grad_keyneg = (weight_neg * renewed * factor).astype(BF)
        grad_cand = grad_renewed * (1.0 - update) * (1.0 - candidate * candidate)
        grad_reset = (grad_cand * recurrent * reset * (1.0 - reset)).astype(BF)
        grad_update = (
            grad_renewed * (previous - candidate) * update * (1.0 - update)
        ).astype(BF)
        input_back = jnp.concatenate([grad_reset, grad_update, grad_cand.astype(BF)], axis=1)
        renew_grad[t] = grad_renewed * update
        state_grad[t] = jnp.concatenate(
            [grad_reset, grad_update, (grad_cand * reset).astype(BF)], axis=1
        )
        grad_keys = mm_nt(jnp.concatenate([grad_keypos, grad_keyneg], axis=0), wpair[...])
        grad_partner = mm_nt(input_back, win[:width, :]) + grad_keys[:chunk]
        high, low = split(jnp.concatenate([grad_partner, grad_keys[chunk:]], axis=0))
        table_grad[...] += mm(spread[t], high) + mm(spread[t], low)

    high, low = split(table_grad[...])
    for h in range(2):
        back_out[h] = high[:, h * half : (h + 1) * half].reshape(n_node, asked, half)

    def back_copy(h, k):
        peer = to_node(k)
        return pltpu.make_async_remote_copy(
            src_ref=back_out.at[h, peer],
            dst_ref=back_in.at[h, node],
            send_sem=back_send.at[h, peer],
            recv_sem=back_recv.at[h, node],
            device_id=(peer, event),
            device_id_type=MESH,
        )

    def pass_copy(h, slot):
        return to_sibling(
            back_in.at[h, slot],
            back_pair.at[h, slot],
            pass_send.at[h, slot],
            pass_recv.at[h, slot],
        )

    for h in range(2):
        for k in range(n_node - 1, 0, -1):
            back_copy(h, k).start()
    table_grad[...] = low.astype(F32)
    own_low = table_grad[pl.ds(pl.multiple_of(node * asked, asked), asked), :].astype(BF)
    for h in range(2):
        back_in[h, node] = back_out[h, node]
        back_in[h, n_node] = own_low[:, h * half : (h + 1) * half]
        pass_copy(h, node).start()
        pass_copy(h, n_node).start()

    @each_turn(turns)
    def _(t):
        high, low = split(renew_grad[t] + mm_nt(state_grad[t], wst[...]))
        cur[t, 0] = high
        cur[t, 1] = low

    cur_copy = to_sibling(cur, cur_pair, cur_send, cur_recv)
    cur_copy.start()
    arrived_pair = pltpu.make_async_copy(wanted_pair, wanted_pair, list_recv.at[0])
    arrived_pair.wait()
    listed_own = jnp.concatenate([wanted[node]] * 2 + [wanted_pair[node]] * 2, axis=1)
    listed = jnp.concatenate(
        [wanted[to_node(k)] for k in range(1, n_node)]
        + [wanted_pair[to_node(k)] for k in range(1, n_node)],
        axis=1,
    )

    @pl.loop(0, chips)
    def _(j):
        base = (2 * j + core) * block
        place_own[j] = spread_matrix(listed_own, block, base)
        place[j] = spread_matrix(listed, block, base)

    @pl.loop(0, chips)
    def _(j):
        total = jnp.zeros((block, width), F32)
        for t in range(turns):
            at = spread_matrix(source_row[t][:1], block, (2 * j + core) * block)
            total += mm(at, cur[t, 0]) + mm(at, cur[t, 1])
        acc[j] = total

    for h in range(2):
        arrived(back_pair.at[h], pass_recv.at[h], node)
        arrived(back_pair.at[h], pass_recv.at[h], n_node)
    own_rows = jnp.concatenate(
        [
            jnp.concatenate([held[0, at], held[1, at]], axis=1)
            for held in (back_in, back_pair)
            for at in (node, n_node)
        ],
        axis=0,
    )
    pltpu.make_async_copy(source_pair, source_pair, list_recv.at[1]).wait()
    pltpu.make_async_copy(cur_pair, cur_pair, cur_recv).wait()

    @pl.loop(0, chips)
    def _(j):
        total = acc[j] + mm(place_own[j], own_rows)
        for t in range(turns):
            at = spread_matrix(source_pair[t][:1], block, (2 * j + core) * block)
            total += mm(at, cur_pair[t, 0]) + mm(at, cur_pair[t, 1])
        acc[j] = total

    def block_copy(h, j):
        return pltpu.make_async_remote_copy(
            src_ref=block_out.at[h, j],
            dst_ref=block_in.at[h, chip],
            send_sem=block_send.at[h, j],
            recv_sem=block_recv.at[h, chip],
            device_id=(node, 2 * j + core),
            device_id_type=MESH,
        )

    own = []
    for h in range(2):
        for k in range(1, n_node):
            slot = to_node(k)
            arrived(back_in.at[h], back_recv.at[h], slot)
            pass_copy(h, slot).start()
        for k in range(1, n_node):
            arrived(back_pair.at[h], pass_recv.at[h], to_node(k))
        returned = jnp.concatenate(
            [held[h, to_node(k)] for held in (back_in, back_pair) for k in range(1, n_node)],
            axis=0,
        )

        def whole_block(j):
            return acc[j][:, h * half : (h + 1) * half] + mm(place[j], returned)

        @pl.loop(1, chips)
        def _(k):
            j = lax.rem(chip + k, chips)
            block_out[h, j] = whole_block(j).astype(BF)
            block_copy(h, j).start()

        own.append(whole_block(chip))

    for h in range(2):
        total = own[h]
        for k in range(1, chips):
            j = lax.rem(chip + k, chips)
            arrived(block_in.at[h], block_recv.at[h], j)
            total += block_in[h, j].astype(F32)
        out_ref[:, h * half : (h + 1) * half] = total

    for k in range(1, n_node):
        request_copy(k).wait_send()
        table_copy(k).wait_send()
    for h in range(2):
        for k in range(1, n_node):
            back_copy(h, k).wait_send()
        for slot in range(n_node + 1):
            pass_copy(h, slot).wait_send()
        for k in range(1, chips):
            block_copy(h, lax.rem(chip + k, chips)).wait_send()
    wanted_copy.wait_send()
    source_copy.wait_send()
    cur_copy.wait_send()
    for k in range(1, n_node):
        for copy in group_copies(k):
            copy.wait_send()

    @pl.loop(1, n_event)
    def _(k):
        for copy in owner_copies(k):
            copy.wait_send()


def local(
    memory,
    event_feat,
    event_source,
    event_partner,
    event_negative,
    event_time,
    event_count,
    requests,
    w_input,
    w_state,
    w_pair,
    gate_bias,
    time_freq,
):
    n_node = lax.axis_size("node")
    n_event = lax.axis_size("event")
    shards = n_node * n_event
    slots, feat_width = event_feat.shape[2:]
    group_rows, width = memory.shape
    asked = requests.shape[2]
    table_rows = n_node * asked
    events = shards * slots
    chunk = math.gcd(events, 512)
    turns = events // chunk
    chips = n_event // 2
    block = group_rows // n_event
    half = width // 2
    listed = (n_node - 1) * asked
    bias_rows = gate_bias.shape[0] // LANES

    vmem = pl.BlockSpec(memory_space=pltpu.VMEM)
    hbm = pl.BlockSpec(memory_space=pl.ANY)
    dma = pltpu.SemaphoreType.DMA
    ids = [value[0].T for value in (event_source, event_partner, event_negative, event_time)]
    return pl.pallas_call(
        functools.partial(kernel, n_node, n_event, chunk),
        out_shape=OUT((block, width), F32),
        in_specs=[[hbm] * 4] + [hbm] * 9,
        out_specs=vmem,
        scratch_shapes=[
            pltpu.VMEM(memory.shape, BF),
            pltpu.VMEM(w_input.shape, BF),
            pltpu.VMEM(w_state.shape, BF),
            pltpu.VMEM(w_pair.shape, BF),
            pltpu.VMEM((bias_rows, LANES), F32),
            pltpu.VMEM((1, LANES), F32),
            pltpu.VMEM((4, slots, shards), jnp.int32),
            pltpu.VMEM((1, shards), jnp.int32),
            pltpu.VMEM((LANES, max(shards, LANES)), jnp.int32),
            pltpu.VMEM((2 * LANES, 5 * LANES), BF),
            pltpu.VMEM((chunk, 2 * LANES), F32),
            pltpu.VMEM((shards, 1, LANES), jnp.int32),
            pltpu.VMEM((n_node, n_event, slots, feat_width), BF),
            pltpu.VMEM((n_node, n_event, 1, LANES), jnp.int32),
            pltpu.VMEM((n_node, n_event, slots, feat_width), BF),
            pltpu.VMEM((n_node, n_event, 1, LANES), jnp.int32),
            pltpu.VMEM((n_node, 1, asked), jnp.int32),
            pltpu.VMEM((n_node, 1, asked), jnp.int32),
            pltpu.VMEM((n_node, asked, width), BF),
            pltpu.VMEM((n_node, asked, width), BF),
            pltpu.VMEM((turns, chunk, 3 * width), F32),
            pltpu.VMEM((turns, chunk, width), F32),
            pltpu.VMEM((turns, chunk, width), BF),
            pltpu.VMEM((turns, 2, 8, chunk), jnp.int32),
            pltpu.VMEM((turns, 8, chunk), jnp.int32),
            pltpu.VMEM((turns, 8, chunk), jnp.int32),
            pltpu.VMEM((turns, chunk, LANES), F32),
            pltpu.VMEM((turns, chunk, LANES), BF),
            pltpu.VMEM((turns, 2 * chunk, table_rows), BF),
            pltpu.VMEM((turns, table_rows, 2 * chunk), BF),
            pltpu.VMEM((chips, block, 4 * asked), BF),
            pltpu.VMEM((chips, block, 2 * listed), BF),
            pltpu.VMEM((table_rows, width), F32),
            pltpu.VMEM((turns, chunk, width), F32),
            pltpu.VMEM((turns, chunk, 3 * width), BF),
            pltpu.VMEM((turns, 2, chunk, width), BF),
            pltpu.VMEM((turns, 2, chunk, width), BF),
            pltpu.VMEM((2, n_node, asked, half), BF),
            pltpu.VMEM((2, n_node + 1, asked, half), BF),
            pltpu.VMEM((2, n_node + 1, asked, half), BF),
            pltpu.VMEM((chips, block, width), F32),
            pltpu.VMEM((2, chips, block, half), BF),
            pltpu.VMEM((2, chips, block, half), BF),
            dma((11,)),
            dma((n_node,)),
            dma((n_node,)),
            dma((n_node,)),
            dma((n_node,)),
            dma((n_event,)),
            dma((n_event,)),
            dma((n_event,)),
            dma((n_event,)),
            dma((n_node,)),
            dma((n_node,)),
            dma((n_node,)),
            dma((n_node,)),
            dma((2,)),
            dma((2,)),
            dma,
            dma,
            dma((2, n_node)),
            dma((2, n_node)),
            dma((2, n_node + 1)),
            dma((2, n_node + 1)),
            dma((2, chips)),
            dma((2, chips)),
        ],
        compiler_params=pltpu.CompilerParams(
            collective_id=0, has_side_effects=True, vmem_limit_bytes=60 * 1024 * 1024
        ),
        name="memory_step",
    )(
        ids,
        event_count,
        event_feat[0],
        requests[0][:, None, :],
        memory,
        w_input,
        w_state,
        w_pair,
        gate_bias.reshape(bias_rows, LANES),
        time_freq[None, :],
    )


def solution(mesh):
    by_device = ("node", "event")
    in_specs = (
        P("node", None),
        P(by_device, None, None, None),
        P(by_device, None, None),
        P(by_device, None, None),
        P(by_device, None, None),
        P(by_device, None, None),
        P(by_device, None),
        P(by_device, None, None),
        P(),
        P(),
        P(),
        P(),
        P(),
    )
    out_specs = P(by_device, None)
    return jax.shard_map(local, mesh=mesh, in_specs=in_specs, out_specs=out_specs, check_vma=False)
```
